32 devices in a mesh: pipe: 2 (over core), group: 4 (over y, x), local: 4 (over z).
Axes of the slice: x: 2, y: 2, z: 4, core: 2. Of those that a mesh axis runs over, the one named last changes fastest.
Arguments:
- output_grad: bfloat16 [2, 512, 2048], P(None, ('group', 'local')), may hold values from -6 to 6
- carried_grad: bfloat16 [512, 2048], P(('group', 'local')), may hold values from -6 to 6
- layer_inputs: bfloat16 [2, 2, 512, 2048], P('pipe', None, ('group', 'local')), may hold values from -6 to 6
- expert_ids: int32 [2, 2, 512, 6], P('pipe', None, ('group', 'local')), may hold values from 0 to 7, all different within a row; in each aligned block of 32 rows (0 to 31, 32 to 63, ..., all dimensions but the last counted through in order) at most 32 rows name the same one
- gate_prob: bfloat16 [2, 2, 512, 6], P('pipe', None, ('group', 'local')), may hold values from 0.099609375 to 0.796875
- gate_weight: bfloat16 [2, 16, 2048, 704], P('pipe', ('group', 'local')), may hold values from -0.125 to 0.125
- up_weight: bfloat16 [2, 16, 2048, 704], P('pipe', ('group', 'local')), may hold values from -0.125 to 0.125
- down_weight: bfloat16 [2, 16, 704, 2048], P('pipe', ('group', 'local')), may hold values from -0.15625 to 0.15625
Outputs:
- input_grad: bfloat16 [2, 2, 512, 2048], P('pipe', None, ('group', 'local'))
- gate_grad: bfloat16 [2, 2, 512, 6], P('pipe', None, ('group', 'local'))
The draws below stay inside these ranges and needn't reach their ends.
Inputs may be any that keep to these rules, and one draw needn't show every extreme that they name: `expert_ids`: each token names 6 different experts. Within each section and microbatch, the 32 tokens of one device (aligned blocks of rows) name any one expert at most 32 times.
All inputs are finite; a program needn't handle non-finite values.
Results may differ from the reference program's by a relative error of at most 0.0065.
Values may be sent and summed in bfloat16 or wider, within the bound.
No kernel may reach another device: no remote copies, remote signals or barrier semaphores. Data moves between devices by JAX's collectives and lax.ppermute only.
A program may use at most 128 MiB of HBM per device.

```python
import math
import jax
import jax.numpy as jnp
import numpy as np
from jax import lax

D = 2048
FF = 1408
TOP = 6
TOK_DEV = 32
MICRO = 2
SECTIONS = 2
EXPERTS = 8
ECAP = 32
TOKENS = 512


def block_scale(own_key, shape, pieces, least, top_value):
    loudness = 1.0
    for axis_at, parts in pieces:
        draws = jax.random.uniform(jax.random.fold_in(jax.random.fold_in(own_key, 6), axis_at), (parts,), jnp.float32, least / len(pieces), top_value / len(pieces))
        loudness = loudness * jnp.repeat(jnp.exp(draws), shape[axis_at] // parts).reshape((-1,) + (1,) * (len(shape) - 1 - axis_at))
    return loudness


def shared_out(own_key, own, number, rows, amount, top, bound, slope):
    ranking = jax.random.permutation(own_key, amount)
    crowded, usual = shares(amount, rows * top, bound, slope, True), shares(amount, rows * top, bound, slope, False)
    places = jnp.arange(amount)

    def named(sizes, offset_by):
        used = int((sizes > 0).sum())
        fixed = max(1, used // 4)
        shifted = fixed + (places - fixed + offset_by * (used - fixed)) % max(1, amount - fixed)
        return jnp.zeros((amount,), jnp.int32).at[ranking[jnp.where(places < fixed, places, shifted)]].set(jnp.asarray(sizes, jnp.int32))

    sizes = jnp.where(number % 4 == 0, named(crowded, number // 4), named(usual, number - number // 4 - 1))
    mixed = jax.random.permutation(jax.random.fold_in(own, 3), amount)
    giver, receiver = mixed[0:amount // 2 * 2:2], mixed[1:amount // 2 * 2:2]
    room = jnp.minimum(sizes[giver] - 1, bound - sizes[receiver]) // 2
    room = jnp.where((giver == ranking[0]) | (receiver == ranking[0]) | (sizes[receiver] == 0), 0, jnp.maximum(room, 0))
    shifted = jax.random.randint(jax.random.fold_in(own, 4), (amount // 2,), 0, 1 << 20) % (room + 1)
    sizes = sizes.at[giver].add(-shifted).at[receiver].add(shifted)
    labels = jnp.searchsorted(jnp.cumsum(sizes), jnp.arange(rows * top), side="right").astype(jnp.int32)
    table = labels.reshape(top, rows).T
    table = table[jax.random.permutation(jax.random.fold_in(own, 1), rows)]
    offset_by = jax.random.randint(jax.random.fold_in(own, 2), (rows, 1), 0, top)
    return jnp.take_along_axis(table, (jnp.arange(top)[None, :] + offset_by) % top, axis=1)


def shares(number_of, total, bound, slope, full):
    loads = [(1 << 20) // math.isqrt(grade ** slope) + 1 for grade in range(1, number_of + 1)]
    largest = bound if full else min(bound, max(-(-total // number_of), total * loads[0] // sum(loads)))
    least = 1 if total - largest >= number_of - 1 else 0
    given, rest = [largest] + [least] * (number_of - 1), total - largest - least * (number_of - 1)
    while rest > 0:
        free = [i for i in range(1, number_of) if given[i] < largest] or [i for i in range(1, number_of) if given[i] < bound]
        pool, left = sum([loads[i] for i in free]), rest
        for i in free:
            addition = min(bound - given[i], max(1, left * loads[i] // pool), rest)
            given[i] = given[i] + addition
            rest = rest - addition
    return np.array(given)


def noise(stream_key, shape, deviation, limit, shards=(), held_as=jnp.bfloat16):
    level = block_scale(stream_key, shape, shards, -0.22, 0.18) if shards else 1.0
    values = jax.random.normal(stream_key, shape, jnp.float32) * deviation * level
    return jnp.minimum(jnp.maximum(values, -limit), limit).astype(held_as)


def setup_inputs(seed: int = 0) -> dict:
    arg_keys = jax.random.split(jax.random.key(seed), 9)
    output_grad = noise(arg_keys[0], (MICRO, TOKENS, D), 1.0, 6.0, ((1, 16),))
    carried_grad = noise(arg_keys[1], (TOKENS, D), 1.0, 6.0, ((0, 16),))
    layer_inputs = noise(arg_keys[2], (SECTIONS, MICRO, TOKENS, D), 1.0, 6.0, ((0, 2), (2, 16)))
    expert_ids_keys = jax.random.split(jax.random.fold_in(arg_keys[3], 1), SECTIONS * MICRO * TOKENS // TOK_DEV)
    expert_ids_turns = jax.random.permutation(jax.random.fold_in(arg_keys[3], 3), SECTIONS * MICRO * TOKENS // TOK_DEV)
    expert_ids = jax.vmap(lambda own, number: shared_out(jax.random.fold_in(arg_keys[3], 2), own, number, TOK_DEV, EXPERTS, TOP, ECAP, 1))(expert_ids_keys, expert_ids_turns).reshape((SECTIONS, MICRO, TOKENS, TOP))
    gate_prob = jnp.clip(0.099609375 + 0.6972656 * jax.random.uniform(arg_keys[4], (SECTIONS, MICRO, TOKENS, TOP), jnp.float32) ** block_scale(arg_keys[4], (SECTIONS, MICRO, TOKENS, TOP), ((0, 2), (2, 16)), -0.2, 0.2), 0.099609375, 0.796875).astype(jnp.bfloat16)
    gate_weight = noise(arg_keys[5], (SECTIONS, 2 * EXPERTS, D, FF // 2), D ** -0.5, 0.125, ((0, 2), (1, 16)))
    up_weight = noise(arg_keys[6], (SECTIONS, 2 * EXPERTS, D, FF // 2), D ** -0.5, 0.125, ((0, 2), (1, 16)))
    down_weight = noise(arg_keys[7], (SECTIONS, 2 * EXPERTS, FF // 2, D), FF ** -0.5, 0.15625, ((0, 2), (1, 16)))
    return {"output_grad": output_grad, "carried_grad": carried_grad, "layer_inputs": layer_inputs, "expert_ids": expert_ids, "gate_prob": gate_prob, "gate_weight": gate_weight, "up_weight": up_weight, "down_weight": down_weight}


def expert_backward(rows_in, rows_grad, row_probs, gate_full, up_full, down_full):
    rows_in = rows_in.astype(jnp.float32)
    rows_grad = rows_grad.astype(jnp.float32)
    gate_pre = jnp.dot(rows_in, gate_full.astype(jnp.float32))
    up_pre = jnp.dot(rows_in, up_full.astype(jnp.float32))
    back_proj = jnp.dot(rows_grad, down_full.astype(jnp.float32).T)
    sigmoid_gate = jax.nn.sigmoid(gate_pre)
    activated = gate_pre * sigmoid_gate
    gate_part = jnp.sum(activated * up_pre * back_proj, axis=1)
    scaled = row_probs[:, None] * back_proj
    grad_gate = (scaled * up_pre * sigmoid_gate * (1.0 + gate_pre * (1.0 - sigmoid_gate))).astype(jnp.bfloat16)
    grad_up = (scaled * activated).astype(jnp.bfloat16)
    grad_rows = jnp.dot(grad_gate.astype(jnp.float32), gate_full.astype(jnp.float32).T)
    grad_rows = grad_rows + jnp.dot(grad_up.astype(jnp.float32), up_full.astype(jnp.float32).T)
    return grad_rows, gate_part


def reference(output_grad, carried_grad, layer_inputs, expert_ids, gate_prob, gate_weight, up_weight, down_weight):
    def layer_backward(section_index, micro_index, incoming):
        choices_ids = expert_ids[section_index, micro_index]
        inputs = layer_inputs[section_index, micro_index]
        weights_prob = gate_prob[section_index, micro_index].astype(jnp.float32)
        expert_range = jnp.arange(EXPERTS, dtype=jnp.int32)
        matches = (choices_ids[:, :, None] == expert_range[None, None, :]).astype(jnp.int32)
        chosen = jnp.sum(matches, axis=1)
        before = jnp.cumsum(chosen, axis=0) - chosen
        position = jnp.sum(matches * before[:, None, :], axis=2).astype(jnp.int32)
        capacity_rows = (TOKENS // TOK_DEV) * ECAP
        token_index = jnp.broadcast_to(jnp.arange(TOKENS, dtype=jnp.int32)[:, None], choices_ids.shape)
        index_table = jnp.zeros((EXPERTS, capacity_rows), jnp.int32).at[choices_ids, position].set(token_index)
        prob_table = jnp.zeros((EXPERTS, capacity_rows), jnp.float32).at[choices_ids, position].set(weights_prob)
        gate_halves = gate_weight[section_index].reshape(EXPERTS, 2, D, FF // 2)
        up_halves = up_weight[section_index].reshape(EXPERTS, 2, D, FF // 2)
        down_halves = down_weight[section_index].reshape(EXPERTS, 2, FF // 2, D)

        def per_expert(operands):
            index_row, prob_row, gate_pair, up_pair, down_pair = operands
            gate_full = jnp.concatenate([gate_pair[0], gate_pair[1]], axis=1)
            up_full = jnp.concatenate([up_pair[0], up_pair[1]], axis=1)
            down_full = jnp.concatenate([down_pair[0], down_pair[1]], axis=0)
            grad_rows, gate_part = expert_backward(inputs[index_row], incoming[index_row], prob_row, gate_full, up_full, down_full)
            return grad_rows.astype(jnp.bfloat16), gate_part.astype(jnp.bfloat16)

        contrib, gate_parts = lax.map(per_expert, (index_table, prob_table, gate_halves, up_halves, down_halves))
        added = jnp.zeros((TOKENS, D), jnp.float32).at[index_table.reshape(-1)].add(contrib.reshape(-1, D).astype(jnp.float32))
        summed = incoming.astype(jnp.float32) + added
        return summed.astype(jnp.bfloat16), gate_parts[choices_ids, position]

    grads_last = []
    gates_last = []
    for micro_index in range(MICRO):
        result_grad, result_gate = layer_backward(1, micro_index, output_grad[micro_index])
        grads_last.append(result_grad)
        gates_last.append(result_gate)
    grads_first = []
    gates_first = []
    for micro_index in range(MICRO):
        if micro_index == 0:
            incoming = carried_grad
        else:
            incoming = grads_last[micro_index - 1]
        result_grad, result_gate = layer_backward(0, micro_index, incoming)
        grads_first.append(result_grad)
        gates_first.append(result_gate)
    input_grad = jnp.stack([jnp.stack(grads_first), jnp.stack(grads_last)])
    gate_grad = jnp.stack([jnp.stack(gates_first), jnp.stack(gates_last)])
    return input_grad, gate_grad
```

```python
import functools

import jax
import jax.numpy as jnp
from jax import lax
from jax.experimental import pallas as pl
from jax.experimental.pallas import tpu as pltpu
from jax.sharding import PartitionSpec as P

CONTRACT_LAST = (((1,), (1,)), ((), ()))
CONTRACT_FIRST = (((0,), (0,)), ((), ()))


def swapped(value, axis, bit):
    mask = 2**bit
    pairs = [(source, source ^ mask) for source in range(lax.axis_size(axis))]
    return lax.ppermute(value, axis, pairs)


def from_behind(block, axis, distance):
    devices = range(lax.axis_size(axis))
    route = [(i - distance, i) for i in devices if i - distance in devices]
    return lax.ppermute(block, axis, route)


def expert_backward(rows_in, rows_grad, row_probs, gate_full, up_full, down_full):
    gate_pre = jnp.dot(rows_in, gate_full, preferred_element_type=jnp.float32)
    up_pre = jnp.dot(rows_in, up_full, preferred_element_type=jnp.float32)
    back_proj = lax.dot_general(
        rows_grad, down_full, CONTRACT_LAST, preferred_element_type=jnp.float32
    )
    sigmoid_gate = jax.nn.sigmoid(gate_pre)
    activated = gate_pre * sigmoid_gate
    gate_part = jnp.sum(activated * up_pre * back_proj, axis=1)
    scaled = row_probs.astype(jnp.float32)[:, None] * back_proj
    grad_gate = (scaled * up_pre * sigmoid_gate * (1.0 + gate_pre * (1.0 - sigmoid_gate))).astype(
        jnp.bfloat16
    )
    grad_up = (scaled * activated).astype(jnp.bfloat16)
    grad_rows = lax.dot_general(
        grad_gate, gate_full, CONTRACT_LAST, preferred_element_type=jnp.float32
    )
    grad_rows = grad_rows + lax.dot_general(
        grad_up, up_full, CONTRACT_LAST, preferred_element_type=jnp.float32
    )
    return (grad_rows, gate_part)


def route_tables(choice_ids, choice_probs, expert_count, capacity):
    expert_range = jnp.arange(expert_count, dtype=jnp.int32)
    matches = (choice_ids[:, :, None] == expert_range[None, None, :]).astype(jnp.int32)
    chosen = jnp.sum(matches, axis=1)
    rows = jnp.arange(choice_ids.shape[0])
    earlier = (rows[:, None] > rows[None, :]).astype(jnp.float32)
    before = jnp.dot(earlier, chosen.astype(jnp.float32)).astype(jnp.int32)
    slot_range = jnp.arange(capacity, dtype=jnp.int32)
    placed = (before[:, :, None] == slot_range[None, None, :]) & (chosen[:, :, None] > 0)
    slot_map = jnp.transpose(placed, (1, 2, 0)).astype(jnp.float32)
    token_probs = jnp.sum(
        matches.astype(jnp.float32) * choice_probs.astype(jnp.float32)[:, :, None], axis=1
    )
    slot_probs = jnp.einsum("ect,te->ec", slot_map, token_probs)
    return (matches, slot_map, slot_probs)


def layer_backward(incoming, inputs, choice_ids, choice_probs, weights_local, expert_count):
    tokens_here = incoming.shape[0]
    model_width = incoming.shape[1]
    top_count = choice_ids.shape[1]
    capacity = 2 * ((tokens_here * top_count * 2 + 3 * expert_count - 1) // (3 * expert_count))
    half_slots = capacity // 2
    devices = 2 * expert_count
    matches, slot_map, slot_probs = route_tables(choice_ids, choice_probs, expert_count, capacity)
    flat_map = slot_map.reshape(expert_count * capacity, tokens_here).astype(jnp.bfloat16)
    sent_inputs = jnp.dot(flat_map, inputs, preferred_element_type=jnp.float32).astype(jnp.bfloat16)
    sent_grads = jnp.dot(flat_map, incoming, preferred_element_type=jnp.float32).astype(
        jnp.bfloat16
    )
    sent_probs = slot_probs.reshape(expert_count * capacity).astype(jnp.bfloat16)
    gate_full, up_full, down_full = weights_local
    got_inputs, got_grads, got_probs = (
        lax.all_to_all(sent_inputs, ("group", "local"), split_axis=0, concat_axis=0, tiled=True),
        lax.all_to_all(sent_grads, ("group", "local"), split_axis=0, concat_axis=0, tiled=True),
        lax.all_to_all(sent_probs, ("group", "local"), split_axis=0, concat_axis=0, tiled=True),
    )
    grad_rows, gate_part = expert_backward(
        got_inputs, got_grads, got_probs, gate_full, up_full, down_full
    )
    kept_grad = grad_rows.reshape(devices, half_slots, model_width)
    kept_part = gate_part.reshape(devices, half_slots)
    back_grad, back_part = (
        lax.all_to_all(
            kept_grad.astype(jnp.bfloat16),
            ("group", "local"),
            split_axis=0,
            concat_axis=0,
            tiled=True,
        ),
        lax.all_to_all(
            kept_part.astype(jnp.bfloat16),
            ("group", "local"),
            split_axis=0,
            concat_axis=0,
            tiled=True,
        ),
    )
    back_grad = back_grad.reshape(expert_count * capacity, model_width)
    summed = incoming.astype(jnp.float32) + lax.dot_general(
        flat_map, back_grad, CONTRACT_FIRST, preferred_element_type=jnp.float32
    )
    per_expert = jnp.einsum(
        "ect,ec->te", slot_map, back_part.reshape(expert_count, capacity).astype(jnp.float32)
    )
    gate_values = jnp.sum(matches.astype(jnp.float32) * per_expert[:, None, :], axis=2)
    return (summed.astype(jnp.bfloat16), gate_values.astype(jnp.bfloat16))


def routed_local(
    output_grad,
    carried_grad,
    layer_inputs,
    expert_ids,
    gate_prob,
    gate_weight,
    up_weight,
    down_weight,
):
    expert_count = lax.axis_size("group") * lax.axis_size("local") // 2
    gate_local = gate_weight[0, 0]
    up_local = up_weight[0, 0]
    down_local = down_weight[0, 0]
    gate_other, up_other, down_other = swapped((gate_local, up_local, down_local), "local", 0)
    weights_local = (
        jnp.concatenate([gate_local, gate_other], axis=1),
        jnp.concatenate([up_local, up_other], axis=1),
        jnp.concatenate([down_local, down_other], axis=0),
    )
    last_section = lax.axis_index("pipe") == lax.axis_size("pipe") - 1
    micro_count = output_grad.shape[0]
    grads_out = []
    gates_out = []
    previous = carried_grad
    for micro_index in range(micro_count):
        if micro_index == 0:
            earlier = carried_grad
        else:
            earlier = from_behind(previous, "pipe", -1)
        incoming = jnp.where(last_section, output_grad[micro_index], earlier)
        result_grad, result_gate = layer_backward(
            incoming,
            layer_inputs[0, micro_index],
            expert_ids[0, micro_index],
            gate_prob[0, micro_index],
            weights_local,
            expert_count,
        )
        grads_out.append(result_grad)
        gates_out.append(result_gate)
        previous = result_grad
    return (jnp.stack(grads_out)[None], jnp.stack(gates_out)[None])


VMEM_LIMIT = 56 * 2**20
HIDDEN_TILE = 256
WIDTH_TILE = 256


def tiles(total, step):
    return [(start, min(step, total - start)) for start in range(0, total, step)]


def load_pieces(pieces, target, sems):
    copies = []
    for number, (ref, begin, rows, place) in enumerate(pieces):
        copy = pltpu.make_async_copy(
            ref.at[pl.ds(begin, rows)], target.at[pl.ds(place, rows)], sems.at[number]
        )
        copy.start()
        copies.append(copy)
    for copy in copies:
        copy.wait()


def forward_kernel(plan, *refs):
    count = len(plan)
    piece_refs = refs[:count]
    probs_ref, gate_ref, up_ref, product_ref, gate_factor_ref, up_factor_ref, rows_ref, sems = refs[
        count:
    ]
    load_pieces(
        [(ref,) + place for ref, place in zip(piece_refs, plan)], rows_ref, sems
    )
    rows = rows_ref[...]
    probs = probs_ref[...]
    for start, size in tiles(gate_ref.shape[1], HIDDEN_TILE):
        columns = pl.ds(start, size)
        gate_pre = jnp.dot(rows, gate_ref[:, columns], preferred_element_type=jnp.float32)
        up_pre = jnp.dot(rows, up_ref[:, columns], preferred_element_type=jnp.float32)
        sigmoid_gate = jax.nn.sigmoid(gate_pre)
        activated = gate_pre * sigmoid_gate
        product_ref[:, columns] = activated * up_pre
        up_factor_ref[:, columns] = probs * activated
        gate_factor_ref[:, columns] = (
            probs * up_pre * sigmoid_gate * (1.0 + gate_pre * (1.0 - sigmoid_gate))
        )


def backward_kernel(plan, blocks, *refs):
    count = len(plan)
    piece_refs = refs[:count]
    product_ref, gate_factor_ref, up_factor_ref, gate_ref, up_ref, down_ref = refs[count : count + 6]
    out_refs = refs[count + 6 : count + 6 + len(blocks)]
    part_ref, rows_ref, grad_gate_ref, grad_up_ref, sems = refs[count + 6 + len(blocks) :]
    load_pieces(
        [(ref,) + place for ref, place in zip(piece_refs, plan)], rows_ref, sems
    )
    rows = rows_ref[...]
    part = jnp.zeros(part_ref.shape, jnp.float32)
    for start, size in tiles(down_ref.shape[0], HIDDEN_TILE):
        columns = pl.ds(start, size)
        back_proj = lax.dot_general(
            rows, down_ref[columns, :], CONTRACT_LAST, preferred_element_type=jnp.float32
        )
        part = part + jnp.sum(product_ref[:, columns] * back_proj, axis=1, keepdims=True)
        grad_gate_ref[:, columns] = (gate_factor_ref[:, columns] * back_proj).astype(jnp.bfloat16)
        grad_up_ref[:, columns] = (up_factor_ref[:, columns] * back_proj).astype(jnp.bfloat16)
    part_ref[...] = part
    grad_gate = grad_gate_ref[...]
    grad_up = grad_up_ref[...]
    for start, size in tiles(gate_ref.shape[0], WIDTH_TILE):
        columns = pl.ds(start, size)
        grads = lax.dot_general(
            grad_gate, gate_ref[columns, :], CONTRACT_LAST, preferred_element_type=jnp.float32
        )
        grads = grads + lax.dot_general(
            grad_up, up_ref[columns, :], CONTRACT_LAST, preferred_element_type=jnp.float32
        )
        grads = grads.astype(jnp.bfloat16)
        for out_ref, (place, amount) in zip(out_refs, blocks):
            out_ref[:, columns] = grads[place : place + amount]


ANYWHERE = pl.BlockSpec(memory_space=pl.ANY)
IN_VMEM = pl.BlockSpec(memory_space=pltpu.VMEM)


def forward_part(pieces, plan, probs, gate_half, up_half):
    rows = probs.shape[0]
    width, hidden = gate_half.shape
    factor = jax.ShapeDtypeStruct((rows, hidden), jnp.float32)
    return pl.pallas_call(
        functools.partial(forward_kernel, plan),
        out_shape=(factor, factor, factor),
        in_specs=[ANYWHERE] * len(pieces) + [IN_VMEM] * 3,
        out_specs=(IN_VMEM,) * 3,
        scratch_shapes=[
            pltpu.VMEM((rows, width), jnp.bfloat16),
            pltpu.SemaphoreType.DMA((len(pieces),)),
        ],
        compiler_params=pltpu.CompilerParams(vmem_limit_bytes=VMEM_LIMIT),
        cost_estimate=pl.CostEstimate(
            flops=4 * rows * width * hidden,
            bytes_accessed=4 * width * hidden + 2 * rows * width + 12 * rows * hidden,
            transcendentals=rows * hidden,
        ),
        name="forward_part",
    )(*pieces, probs, gate_half, up_half)


def backward_part(pieces, plan, blocks, factors, gate_half, up_half, down_half):
    rows = factors[0].shape[0]
    width, hidden = gate_half.shape
    outs = [jax.ShapeDtypeStruct((amount, width), jnp.bfloat16) for _, amount in blocks]
    outs.append(jax.ShapeDtypeStruct((rows, 1), jnp.float32))
    return pl.pallas_call(
        functools.partial(backward_kernel, plan, blocks),
        out_shape=tuple(outs),
        in_specs=[ANYWHERE] * len(pieces) + [IN_VMEM] * 6,
        out_specs=(IN_VMEM,) * len(outs),
        scratch_shapes=[
            pltpu.VMEM((rows, width), jnp.bfloat16),
            pltpu.VMEM((rows, hidden), jnp.bfloat16),
            pltpu.VMEM((rows, hidden), jnp.bfloat16),
            pltpu.SemaphoreType.DMA((len(pieces),)),
        ],
        compiler_params=pltpu.CompilerParams(vmem_limit_bytes=VMEM_LIMIT),
        cost_estimate=pl.CostEstimate(
            flops=6 * rows * width * hidden,
            bytes_accessed=6 * width * hidden + 4 * rows * width + 12 * rows * hidden,
            transcendentals=0,
        ),
        name="backward_part",
    )(*pieces, *factors, gate_half, up_half, down_half)


def toggled(value, axis, mask):
    pairs = [(source, source ^ mask) for source in range(lax.axis_size(axis))]
    return lax.ppermute(value, axis, pairs)


def spread(block):
    near = toggled(block, "local", 1)
    far = toggled(block, "local", 2)
    corner = toggled(far, "local", 1)
    half = block.shape[0] // 2
    found = []
    for column in (block, near, far, corner):
        first = toggled(column, "group", 1)
        second = toggled(column, "group", 2)
        low = toggled(first[:half], "group", 2)
        high = toggled(second[half:], "group", 1)
        found.append((column, first, second, low, high))
    return found


def piece_plan(found, begin, rows):
    half = found[0][0].shape[0] // 2
    arrays, plan = [], []
    for level, (column, first, second, low, high) in enumerate(found):
        for slot, array in ((0, column), (1, first), (2, second)):
            arrays.append(array)
            plan.append((begin, rows, (4 * slot + level) * rows))
        place = (12 + level) * rows
        upto = min(half, begin + rows)
        if begin < upto:
            arrays.append(low)
            plan.append((begin, upto - begin, place))
        since = max(half, begin)
        if since < begin + rows:
            arrays.append(high)
            plan.append((since - half, begin + rows - since, place + since - begin))
    return arrays, tuple(plan)


def added(*values):
    total = values[0].astype(jnp.float32)
    for value in values[1:]:
        total = total + value.astype(jnp.float32)
    return total


def brought_back(blocks, incoming):
    diag_low, diag_high, first_low, first_high, second_low, second_high, own = blocks
    rows = incoming.shape[0]
    got_low = toggled(diag_low, "group", 1)
    got_high = toggled(diag_high, "group", 2)
    from_second_high = toggled(second_high, "group", 2)
    from_first_low = toggled(first_low, "group", 1)
    from_first_high = toggled(added(first_high, got_high).astype(jnp.bfloat16), "group", 1)
    from_second_low = toggled(added(second_low, got_low).astype(jnp.bfloat16), "group", 2)
    high = added(own[2 * rows :], from_first_high, from_second_high)
    low = added(own[: 2 * rows], from_first_low, from_second_low)
    got_corner = toggled(high[rows:].astype(jnp.bfloat16), "local", 1)
    got_far = toggled(added(high[:rows], got_corner).astype(jnp.bfloat16), "local", 2)
    got_near = toggled(low[rows:].astype(jnp.bfloat16), "local", 1)
    return added(incoming, low[:rows], got_near, got_far).astype(jnp.bfloat16)


def by_difference(values):
    own = lax.axis_index("group") * lax.axis_size("local") + lax.axis_index("local")
    count = values.shape[0]
    bit = 1
    while bit < count:
        split = values.reshape((count // (2 * bit), 2, bit) + values.shape[1:])
        flipped = split[:, ::-1].reshape(values.shape)
        values = jnp.where((own & bit) != 0, flipped, values)
        bit *= 2
    return values


def dense_local(
    output_grad,
    carried_grad,
    layer_inputs,
    expert_ids,
    gate_prob,
    gate_weight,
    up_weight,
    down_weight,
):
    devices = lax.axis_size("group") * lax.axis_size("local")
    expert_count = devices // 2
    micro_count, rows = output_grad.shape[:2]
    gate_half, up_half, down_half = gate_weight[0, 0], up_weight[0, 0], down_weight[0, 0]
    everywhere = ("group", "local")
    experts = jnp.arange(expert_count, dtype=jnp.int32)
    matches = (expert_ids[0][..., None] == experts).astype(jnp.float32)
    token_probs = jnp.sum(matches * gate_prob[0].astype(jnp.float32)[..., None], axis=2)
    sent_probs = jnp.repeat(
        jnp.transpose(token_probs, (2, 0, 1)).reshape(expert_count, micro_count * rows), 2, axis=0
    )
    got_probs = lax.all_to_all(
        sent_probs.astype(jnp.bfloat16), everywhere, split_axis=0, concat_axis=0, tiled=True
    )
    got_probs = by_difference(got_probs.astype(jnp.float32)).reshape(devices, micro_count, rows)
    slot_probs = [got_probs[:, m].reshape(devices * rows, 1) for m in range(micro_count)]
    last_section = lax.axis_index("pipe") == lax.axis_size("pipe") - 1
    inputs = layer_inputs[0]
    quarter = 4 * rows
    blocks = (
        (3 * quarter, 2 * rows),
        (3 * quarter + 2 * rows, 2 * rows),
        (quarter, 2 * rows),
        (quarter + 2 * rows, 2 * rows),
        (2 * quarter, 2 * rows),
        (2 * quarter + 2 * rows, 2 * rows),
        (0, quarter),
    )
    incoming = jnp.where(last_section, output_grad[0], carried_grad)
    found = spread(jnp.concatenate([inputs[0], incoming], axis=0))
    factors = []
    grads_pieces = piece_plan(found, rows, rows)
    arrays, plan = piece_plan(found, 0, rows)
    factors.append(forward_part(arrays, plan, slot_probs[0], gate_half, up_half))
    later = inputs[1:]
    found[-1], later = lax.optimization_barrier((found[-1], later))
    for m in range(1, micro_count):
        arrays, plan = piece_plan(spread(later[m - 1]), 0, rows)
        factors.append(forward_part(arrays, plan, slot_probs[m], gate_half, up_half))
    grads_out, parts = [], []
    for m in range(micro_count):
        if m > 0:
            earlier = from_behind(grads_out[-1], "pipe", -1)
            incoming = jnp.where(last_section, output_grad[m], earlier)
            grads_pieces = piece_plan(spread(incoming), 0, rows)
        *pieces, part = backward_part(
            *grads_pieces, blocks, factors[m], gate_half, up_half, down_half
        )
        grads_out.append(brought_back(pieces, incoming))
        parts.append(
            lax.all_to_all(
                by_difference(part.reshape(devices, rows)),
                everywhere,
                split_axis=0,
                concat_axis=0,
                tiled=True,
            )
        )
    per_expert = jnp.stack(parts).reshape(micro_count, expert_count, 2, rows).sum(axis=2)
    gates = jnp.sum(matches * jnp.transpose(per_expert, (0, 2, 1))[:, :, None, :], axis=3)
    return (jnp.stack(grads_out)[None], gates.astype(jnp.bfloat16)[None])


def local(*arguments):
    group, ring = lax.axis_size("group"), lax.axis_size("local")
    top_count = arguments[3].shape[-1]
    expert_count = group * ring // 2
    crowded = 3 * expert_count <= 4 * top_count
    if group == 4 and ring == 4 and crowded:
        return dense_local(*arguments)
    return routed_local(*arguments)


def solution(mesh):
    return jax.shard_map(
        local,
        mesh=mesh,
        in_specs=(
            P(None, ("group", "local"), None),
            P(("group", "local"), None),
            P("pipe", None, ("group", "local"), None),
            P("pipe", None, ("group", "local"), None),
            P("pipe", None, ("group", "local"), None),
            P("pipe", ("group", "local"), None, None),
            P("pipe", ("group", "local"), None, None),
            P("pipe", ("group", "local"), None, None),
        ),
        out_specs=(
            P("pipe", None, ("group", "local"), None),
            P("pipe", None, ("group", "local"), None),
        ),
        check_vma=False,
    )
```

```python
import functools

import jax
import jax.numpy as jnp
from jax import lax
from jax.experimental import pallas as pl
from jax.experimental.pallas import tpu as pltpu
from jax.sharding import PartitionSpec as P

CONTRACT_LAST = (((1,), (1,)), ((), ()))
CONTRACT_FIRST = (((0,), (0,)), ((), ()))


def swapped(value, axis, bit):
    mask = 2**bit
    pairs = [(source, source ^ mask) for source in range(lax.axis_size(axis))]
    return lax.ppermute(value, axis, pairs)


def from_behind(block, axis, distance):
    devices = range(lax.axis_size(axis))
    route = [(i - distance, i) for i in devices if i - distance in devices]
    return lax.ppermute(block, axis, route)


def expert_backward(rows_in, rows_grad, row_probs, gate_full, up_full, down_full):
    gate_pre = jnp.dot(rows_in, gate_full, preferred_element_type=jnp.float32)
    up_pre = jnp.dot(rows_in, up_full, preferred_element_type=jnp.float32)
    back_proj = lax.dot_general(
        rows_grad, down_full, CONTRACT_LAST, preferred_element_type=jnp.float32
    )
    sigmoid_gate = jax.nn.sigmoid(gate_pre)
    activated = gate_pre * sigmoid_gate
    gate_part = jnp.sum(activated * up_pre * back_proj, axis=1)
    scaled = row_probs.astype(jnp.float32)[:, None] * back_proj
    grad_gate = (scaled * up_pre * sigmoid_gate * (1.0 + gate_pre * (1.0 - sigmoid_gate))).astype(
        jnp.bfloat16
    )
    grad_up = (scaled * activated).astype(jnp.bfloat16)
    grad_rows = lax.dot_general(
        grad_gate, gate_full, CONTRACT_LAST, preferred_element_type=jnp.float32
    )
    grad_rows = grad_rows + lax.dot_general(
        grad_up, up_full, CONTRACT_LAST, preferred_element_type=jnp.float32
    )
    return (grad_rows, gate_part)


def route_tables(choice_ids, choice_probs, expert_count, capacity):
    expert_range = jnp.arange(expert_count, dtype=jnp.int32)
    matches = (choice_ids[:, :, None] == expert_range[None, None, :]).astype(jnp.int32)
    chosen = jnp.sum(matches, axis=1)
    rows = jnp.arange(choice_ids.shape[0])
    earlier = (rows[:, None] > rows[None, :]).astype(jnp.float32)
    before = jnp.dot(earlier, chosen.astype(jnp.float32)).astype(jnp.int32)
    slot_range = jnp.arange(capacity, dtype=jnp.int32)
    placed = (before[:, :, None] == slot_range[None, None, :]) & (chosen[:, :, None] > 0)
    slot_map = jnp.transpose(placed, (1, 2, 0)).astype(jnp.float32)
    token_probs = jnp.sum(
        matches.astype(jnp.float32) * choice_probs.astype(jnp.float32)[:, :, None], axis=1
    )
    slot_probs = jnp.einsum("ect,te->ec", slot_map, token_probs)
    return (matches, slot_map, slot_probs)


def layer_backward(incoming, inputs, choice_ids, choice_probs, weights_local, expert_count):
    tokens_here = incoming.shape[0]
    model_width = incoming.shape[1]
    top_count = choice_ids.shape[1]
    capacity = 2 * ((tokens_here * top_count * 2 + 3 * expert_count - 1) // (3 * expert_count))
    half_slots = capacity // 2
    devices = 2 * expert_count
    matches, slot_map, slot_probs = route_tables(choice_ids, choice_probs, expert_count, capacity)
    flat_map = slot_map.reshape(expert_count * capacity, tokens_here).astype(jnp.bfloat16)
    sent_inputs = jnp.dot(flat_map, inputs, preferred_element_type=jnp.float32).astype(jnp.bfloat16)
    sent_grads = jnp.dot(flat_map, incoming, preferred_element_type=jnp.float32).astype(
        jnp.bfloat16
    )
    sent_probs = slot_probs.reshape(expert_count * capacity).astype(jnp.bfloat16)
    gate_full, up_full, down_full = weights_local
    got_inputs, got_grads, got_probs = (
        lax.all_to_all(sent_inputs, ("group", "local"), split_axis=0, concat_axis=0, tiled=True),
        lax.all_to_all(sent_grads, ("group", "local"), split_axis=0, concat_axis=0, tiled=True),
        lax.all_to_all(sent_probs, ("group", "local"), split_axis=0, concat_axis=0, tiled=True),
    )
    grad_rows, gate_part = expert_backward(
        got_inputs, got_grads, got_probs, gate_full, up_full, down_full
    )
    kept_grad = grad_rows.reshape(devices, half_slots, model_width)
    kept_part = gate_part.reshape(devices, half_slots)
    back_grad, back_part = (
        lax.all_to_all(
            kept_grad.astype(jnp.bfloat16),
            ("group", "local"),
            split_axis=0,
            concat_axis=0,
            tiled=True,
        ),
        lax.all_to_all(
            kept_part.astype(jnp.bfloat16),
            ("group", "local"),
            split_axis=0,
            concat_axis=0,
            tiled=True,
        ),
    )
    back_grad = back_grad.reshape(expert_count * capacity, model_width)
    summed = incoming.astype(jnp.float32) + lax.dot_general(
        flat_map, back_grad, CONTRACT_FIRST, preferred_element_type=jnp.float32
    )
    per_expert = jnp.einsum(
        "ect,ec->te", slot_map, back_part.reshape(expert_count, capacity).astype(jnp.float32)
    )
    gate_values = jnp.sum(matches.astype(jnp.float32) * per_expert[:, None, :], axis=2)
    return (summed.astype(jnp.bfloat16), gate_values.astype(jnp.bfloat16))


def routed_local(
    output_grad,
    carried_grad,
    layer_inputs,
    expert_ids,
    gate_prob,
    gate_weight,
    up_weight,
    down_weight,
):
    expert_count = lax.axis_size("group") * lax.axis_size("local") // 2
    gate_local = gate_weight[0, 0]
    up_local = up_weight[0, 0]
    down_local = down_weight[0, 0]
    gate_other, up_other, down_other = swapped((gate_local, up_local, down_local), "local", 0)
    weights_local = (
        jnp.concatenate([gate_local, gate_other], axis=1),
        jnp.concatenate([up_local, up_other], axis=1),
        jnp.concatenate([down_local, down_other], axis=0),
    )
    last_section = lax.axis_index("pipe") == lax.axis_size("pipe") - 1
    micro_count = output_grad.shape[0]
    grads_out = []
    gates_out = []
    previous = carried_grad
    for micro_index in range(micro_count):
        if micro_index == 0:
            earlier = carried_grad
        else:
            earlier = from_behind(previous, "pipe", -1)
        incoming = jnp.where(last_section, output_grad[micro_index], earlier)
        result_grad, result_gate = layer_backward(
            incoming,
            layer_inputs[0, micro_index],
            expert_ids[0, micro_index],
            gate_prob[0, micro_index],
            weights_local,
            expert_count,
        )
        grads_out.append(result_grad)
        gates_out.append(result_gate)
        previous = result_grad
    return (jnp.stack(grads_out)[None], jnp.stack(gates_out)[None])


VMEM_LIMIT = 58 * 2**20
WIDTH_TILE = 512
LANES = 128


def tiles(total, step):
    return [(start, min(step, total - start)) for start in range(0, total, step)]


def whole_lanes(amount):
    return (amount + LANES - 1) // LANES * LANES


def begun(source, target, sem):
    copy = pltpu.make_async_copy(source, target, sem)
    copy.start()
    return copy


def pieces_begun(piece_refs, plan, rows_ref, sems):
    return [
        begun(
            ref.at[pl.ds(begin, rows), pl.ds(0, rows_ref.shape[1])],
            rows_ref.at[pl.ds(place, rows)],
            sems.at[number],
        )
        for number, (ref, (begin, rows, place)) in enumerate(zip(piece_refs, plan))
    ]


def both_begun(gate_hbm, up_hbm, both_ref, sems):
    hidden = gate_hbm.shape[0]
    padded = both_ref.shape[0] // 2
    return [
        begun(gate_hbm, both_ref.at[pl.ds(0, hidden)], sems.at[0]),
        begun(up_hbm, both_ref.at[pl.ds(padded, hidden)], sems.at[1]),
    ]


def math_kernel(plan, grad_plan, blocks, expert_ref, *refs):
    count, grad_count = len(plan), len(grad_plan)
    row_refs, grad_refs = refs[:count], refs[count : count + grad_count]
    gate_hbm, up_hbm, down_hbm = refs[count + grad_count : count + grad_count + 3]
    refs = refs[count + grad_count + 3 :]
    out_refs, refs = refs[: len(blocks)], refs[len(blocks) :]
    rows_ref, grad_rows_ref, down_ref, both_ref, grads_ref = refs[:5]
    piece_sems, grad_sems, sems, both_sems = refs[5:]
    hidden, width = down_ref.shape
    padded = both_ref.shape[0] // 2
    copies = pieces_begun(row_refs, plan, rows_ref, piece_sems)
    copies += both_begun(gate_hbm, up_hbm, both_ref, both_sems)
    late_copies = pieces_begun(grad_refs, grad_plan, grad_rows_ref, grad_sems)
    late_copies.append(begun(down_hbm, down_ref, sems.at[0]))
    for start in (hidden, padded + hidden):
        both_ref[pl.ds(start, padded - hidden), :] = jnp.zeros(
            (padded - hidden, width), jnp.bfloat16
        )
        grads_ref[:, pl.ds(start, padded - hidden)] = jnp.zeros(
            (grads_ref.shape[0], padded - hidden), jnp.bfloat16
        )
    for copy in copies:
        copy.wait()
    pre = lax.dot_general(
        rows_ref[...], both_ref[...], CONTRACT_LAST, preferred_element_type=jnp.float32
    )
    gate_pre, up_pre = pre[:, :hidden], pre[:, padded : padded + hidden]
    for copy in late_copies:
        copy.wait()
    back_proj = lax.dot_general(
        grad_rows_ref[:, :width], down_ref[...], CONTRACT_LAST, preferred_element_type=jnp.float32
    )
    lanes = lax.broadcasted_iota(jnp.int32, (1, LANES), 1)
    mine = lanes == expert_ref[0]
    probs = jnp.sum(
        jnp.where(mine, grad_rows_ref[:, width:].astype(jnp.float32), 0.0), axis=1, keepdims=True
    )
    sigmoid_gate = jax.nn.sigmoid(gate_pre)
    activated = gate_pre * sigmoid_gate
    scaled = probs * back_proj
    grads_ref[:, :hidden] = (
        scaled * up_pre * sigmoid_gate * (1.0 + gate_pre * (1.0 - sigmoid_gate))
    ).astype(jnp.bfloat16)
    grads_ref[:, pl.ds(padded, hidden)] = (scaled * activated).astype(jnp.bfloat16)
    part = jnp.sum(activated * up_pre * back_proj, axis=1, keepdims=True)
    part = jnp.where(mine, part, 0.0).astype(jnp.bfloat16)
    for out_ref, (place, amount) in zip(out_refs, blocks):
        out_ref[:, width:] = part[place : place + amount]
    for start, size in tiles(width, WIDTH_TILE):
        columns = pl.ds(start, size)
        grads = jnp.dot(
            grads_ref[...], both_ref[:, columns], preferred_element_type=jnp.float32
        ).astype(jnp.bfloat16)
        for out_ref, (place, amount) in zip(out_refs, blocks):
            out_ref[:, columns] = grads[place : place + amount]


ANYWHERE = pl.BlockSpec(memory_space=pl.ANY)
IN_VMEM = pl.BlockSpec(memory_space=pltpu.VMEM)


def expert_math(rows_in, plan, grads_in, grad_plan, blocks, expert, weights):
    hidden, width = weights[0].shape
    rows = sum(amount for _, amount in blocks)
    outs = [jax.ShapeDtypeStruct((amount, width + LANES), jnp.bfloat16) for _, amount in blocks]
    return pl.pallas_call(
        functools.partial(math_kernel, plan, grad_plan, blocks),
        out_shape=tuple(outs),
        in_specs=[pl.BlockSpec(memory_space=pltpu.SMEM)]
        + [ANYWHERE] * (len(rows_in) + len(grads_in) + 3),
        out_specs=(IN_VMEM,) * len(outs),
        scratch_shapes=[
            pltpu.VMEM((rows, width), jnp.bfloat16),
            pltpu.VMEM((rows, width + LANES), jnp.bfloat16),
            pltpu.VMEM((hidden, width), jnp.bfloat16),
            pltpu.VMEM((2 * whole_lanes(hidden), width), jnp.bfloat16),
            pltpu.VMEM((rows, 2 * whole_lanes(hidden)), jnp.bfloat16),
            pltpu.SemaphoreType.DMA((len(rows_in),)),
            pltpu.SemaphoreType.DMA((len(grads_in),)),
            pltpu.SemaphoreType.DMA((1,)),
            pltpu.SemaphoreType.DMA((2,)),
        ],
        compiler_params=pltpu.CompilerParams(vmem_limit_bytes=VMEM_LIMIT),
        cost_estimate=pl.CostEstimate(
            flops=10 * rows * width * hidden,
            bytes_accessed=6 * width * hidden + 6 * rows * width,
            transcendentals=rows * hidden,
        ),
        name="expert_math",
    )(expert, *rows_in, *grads_in, *weights)


def toggled(value, axis, mask):
    pairs = [(source, source ^ mask) for source in range(lax.axis_size(axis))]
    return lax.ppermute(value, axis, pairs)


def spread(block):
    near = toggled(block, "local", 1)
    far = toggled(block, "local", 2)
    first = [toggled(block, "group", 1)]
    second = [toggled(block, "group", 2)]
    corner = toggled(far, "local", 1)
    first += [toggled(column, "group", 1) for column in (far, corner)]
    second += [toggled(column, "group", 2) for column in (far, corner)]
    first.insert(1, toggled(first[0], "local", 1))
    second.insert(1, toggled(second[0], "local", 1))
    half = block.shape[0] // 2
    low = [toggled(column[:half], "group", 2) for column in first]
    high = [toggled(column[half:], "group", 1) for column in second]
    return list(zip((block, near, far, corner), first, second, low, high))


def piece_plan(found, begin, rows):
    half = found[0][0].shape[0] // 2
    arrays, plan = [], []
    for level, (column, first, second, low, high) in enumerate(found):
        for slot, array in ((0, column), (1, first), (2, second)):
            arrays.append(array)
            plan.append((begin, rows, (4 * slot + level) * rows))
        place = (12 + level) * rows
        upto = min(half, begin + rows)
        if begin < upto:
            arrays.append(low)
            plan.append((begin, upto - begin, place))
        since = max(half, begin)
        if since < begin + rows:
            arrays.append(high)
            plan.append((since - half, begin + rows - since, place + since - begin))
    return arrays, tuple(plan)


def added(*values):
    total = values[0].astype(jnp.float32)
    for value in values[1:]:
        total = total + value.astype(jnp.float32)
    return total


def brought_back(blocks):
    diag_low, diag_high, first_low, first_high, second_low, second_high, own = blocks
    rows = own.shape[0] // 4
    got_low = toggled(diag_low, "group", 1)
    got_high = toggled(diag_high, "group", 2)
    from_second_high = toggled(second_high, "group", 2)
    from_first_low = toggled(first_low, "group", 1)
    from_first_high = toggled(added(first_high, got_high).astype(jnp.bfloat16), "group", 1)
    from_second_low = toggled(added(second_low, got_low).astype(jnp.bfloat16), "group", 2)
    high = added(own[2 * rows :], from_first_high, from_second_high)
    low = added(own[: 2 * rows], from_first_low, from_second_low)
    got_corner = toggled(high[rows:].astype(jnp.bfloat16), "local", 1)
    got_far = toggled(added(high[:rows], got_corner).astype(jnp.bfloat16), "local", 2)
    got_near = toggled(low[rows:].astype(jnp.bfloat16), "local", 1)
    return added(low[:rows], got_near, got_far)


def dense_local(
    output_grad,
    carried_grad,
    layer_inputs,
    expert_ids,
    gate_prob,
    gate_weight,
    up_weight,
    down_weight,
):
    expert_count = lax.axis_size("group") * lax.axis_size("local") // 2
    micro_count, rows, width = output_grad.shape
    gate_half, up_half, down_half = gate_weight[0, 0].T, up_weight[0, 0].T, down_weight[0, 0]
    own_index = lax.axis_index("group") * lax.axis_size("local") + lax.axis_index("local")
    expert = jnp.reshape(own_index // 2, (1,)).astype(jnp.int32)
    matches = (expert_ids[0][..., None] == jnp.arange(LANES, dtype=jnp.int32)).astype(jnp.float32)
    token_probs = jnp.sum(matches * gate_prob[0].astype(jnp.float32)[..., None], axis=2)
    token_probs = token_probs.astype(jnp.bfloat16)
    last_section = lax.axis_index("pipe") == lax.axis_size("pipe") - 1
    inputs = layer_inputs[0]
    quarter = 4 * rows
    blocks = (
        (3 * quarter, 2 * rows),
        (3 * quarter + 2 * rows, 2 * rows),
        (quarter, 2 * rows),
        (quarter + 2 * rows, 2 * rows),
        (2 * quarter, 2 * rows),
        (2 * quarter + 2 * rows, 2 * rows),
        (0, quarter),
    )
    weights = (gate_half, up_half, down_half)
    none = jnp.zeros((rows, LANES), jnp.bfloat16)
    earlier = carried_grad
    grads_out, gates = [], []
    for m in range(micro_count):
        if m > 0:
            earlier = from_behind(grads_out[-1], "pipe", -1)
        incoming = jnp.where(last_section, output_grad[m], earlier)
        sent = jnp.concatenate(
            [
                jnp.concatenate([inputs[m], incoming], axis=0),
                jnp.concatenate([none, token_probs[m]], axis=0),
            ],
            axis=1,
        )
        found = spread(sent)
        arrays, plan = piece_plan(found, 0, rows)
        grad_arrays, grad_plan = piece_plan(found, rows, rows)
        pieces = expert_math(arrays, plan, grad_arrays, grad_plan, blocks, expert, weights)
        total = brought_back(pieces)
        grads_out.append(added(incoming, total[:, :width]).astype(jnp.bfloat16))
        gates.append(total[:, width:])
    gates = jnp.sum(matches * jnp.stack(gates)[:, :, None, :], axis=3).astype(jnp.bfloat16)
    return (jnp.stack(grads_out)[None], gates[None])


def local(*arguments):
    group, ring = lax.axis_size("group"), lax.axis_size("local")
    top_count = arguments[3].shape[-1]
    expert_count = group * ring // 2
    crowded = 3 * expert_count <= 4 * top_count
    if group == 4 and ring == 4 and crowded and expert_count <= LANES:
        return dense_local(*arguments)
    return routed_local(*arguments)


def solution(mesh):
    return jax.shard_map(
        local,
        mesh=mesh,
        in_specs=(
            P(None, ("group", "local"), None),
            P(("group", "local"), None),
            P("pipe", None, ("group", "local"), None),
            P("pipe", None, ("group", "local"), None),
            P("pipe", None, ("group", "local"), None),
            P("pipe", ("group", "local"), None, None),
            P("pipe", ("group", "local"), None, None),
            P("pipe", ("group", "local"), None, None),
        ),
        out_specs=(
            P("pipe", None, ("group", "local"), None),
            P("pipe", None, ("group", "local"), None),
        ),
        check_vma=False,
    )
```

```python
import functools

import jax
import jax.numpy as jnp
from jax import lax
from jax.experimental import pallas as pl
from jax.experimental.pallas import tpu as pltpu
from jax.sharding import PartitionSpec as P

CONTRACT_LAST = (((1,), (1,)), ((), ()))
CONTRACT_FIRST = (((0,), (0,)), ((), ()))


def swapped(value, axis, bit):
    mask = 2**bit
    pairs = [(source, source ^ mask) for source in range(lax.axis_size(axis))]
    return lax.ppermute(value, axis, pairs)


def from_behind(block, axis, distance):
    devices = range(lax.axis_size(axis))
    route = [(i - distance, i) for i in devices if i - distance in devices]
    return lax.ppermute(block, axis, route)


def expert_backward(rows_in, rows_grad, row_probs, gate_full, up_full, down_full):
    gate_pre = jnp.dot(rows_in, gate_full, preferred_element_type=jnp.float32)
    up_pre = jnp.dot(rows_in, up_full, preferred_element_type=jnp.float32)
    back_proj = lax.dot_general(
        rows_grad, down_full, CONTRACT_LAST, preferred_element_type=jnp.float32
    )
    sigmoid_gate = jax.nn.sigmoid(gate_pre)
    activated = gate_pre * sigmoid_gate
    gate_part = jnp.sum(activated * up_pre * back_proj, axis=1)
    scaled = row_probs.astype(jnp.float32)[:, None] * back_proj
    grad_gate = (scaled * up_pre * sigmoid_gate * (1.0 + gate_pre * (1.0 - sigmoid_gate))).astype(
        jnp.bfloat16
    )
    grad_up = (scaled * activated).astype(jnp.bfloat16)
    grad_rows = lax.dot_general(
        grad_gate, gate_full, CONTRACT_LAST, preferred_element_type=jnp.float32
    )
    grad_rows = grad_rows + lax.dot_general(
        grad_up, up_full, CONTRACT_LAST, preferred_element_type=jnp.float32
    )
    return (grad_rows, gate_part)


def route_tables(choice_ids, choice_probs, expert_count, capacity):
    expert_range = jnp.arange(expert_count, dtype=jnp.int32)
    matches = (choice_ids[:, :, None] == expert_range[None, None, :]).astype(jnp.int32)
    chosen = jnp.sum(matches, axis=1)
    rows = jnp.arange(choice_ids.shape[0])
    earlier = (rows[:, None] > rows[None, :]).astype(jnp.float32)
    before = jnp.dot(earlier, chosen.astype(jnp.float32)).astype(jnp.int32)
    slot_range = jnp.arange(capacity, dtype=jnp.int32)
    placed = (before[:, :, None] == slot_range[None, None, :]) & (chosen[:, :, None] > 0)
    slot_map = jnp.transpose(placed, (1, 2, 0)).astype(jnp.float32)
    token_probs = jnp.sum(
        matches.astype(jnp.float32) * choice_probs.astype(jnp.float32)[:, :, None], axis=1
    )
    slot_probs = jnp.einsum("ect,te->ec", slot_map, token_probs)
    return (matches, slot_map, slot_probs)


def layer_backward(incoming, inputs, choice_ids, choice_probs, weights_local, expert_count):
    tokens_here = incoming.shape[0]
    model_width = incoming.shape[1]
    top_count = choice_ids.shape[1]
    capacity = 2 * ((tokens_here * top_count * 2 + 3 * expert_count - 1) // (3 * expert_count))
    half_slots = capacity // 2
    devices = 2 * expert_count
    matches, slot_map, slot_probs = route_tables(choice_ids, choice_probs, expert_count, capacity)
    flat_map = slot_map.reshape(expert_count * capacity, tokens_here).astype(jnp.bfloat16)
    sent_inputs = jnp.dot(flat_map, inputs, preferred_element_type=jnp.float32).astype(jnp.bfloat16)
    sent_grads = jnp.dot(flat_map, incoming, preferred_element_type=jnp.float32).astype(
        jnp.bfloat16
    )
    sent_probs = slot_probs.reshape(expert_count * capacity).astype(jnp.bfloat16)
    gate_full, up_full, down_full = weights_local
    got_inputs, got_grads, got_probs = (
        lax.all_to_all(sent_inputs, ("group", "local"), split_axis=0, concat_axis=0, tiled=True),
        lax.all_to_all(sent_grads, ("group", "local"), split_axis=0, concat_axis=0, tiled=True),
        lax.all_to_all(sent_probs, ("group", "local"), split_axis=0, concat_axis=0, tiled=True),
    )
    grad_rows, gate_part = expert_backward(
        got_inputs, got_grads, got_probs, gate_full, up_full, down_full
    )
    kept_grad = grad_rows.reshape(devices, half_slots, model_width)
    kept_part = gate_part.reshape(devices, half_slots)
    back_grad, back_part = (
        lax.all_to_all(
            kept_grad.astype(jnp.bfloat16),
            ("group", "local"),
            split_axis=0,
            concat_axis=0,
            tiled=True,
        ),
        lax.all_to_all(
            kept_part.astype(jnp.bfloat16),
            ("group", "local"),
            split_axis=0,
            concat_axis=0,
            tiled=True,
        ),
    )
    back_grad = back_grad.reshape(expert_count * capacity, model_width)
    summed = incoming.astype(jnp.float32) + lax.dot_general(
        flat_map, back_grad, CONTRACT_FIRST, preferred_element_type=jnp.float32
    )
    per_expert = jnp.einsum(
        "ect,ec->te", slot_map, back_part.reshape(expert_count, capacity).astype(jnp.float32)
    )
    gate_values = jnp.sum(matches.astype(jnp.float32) * per_expert[:, None, :], axis=2)
    return (summed.astype(jnp.bfloat16), gate_values.astype(jnp.bfloat16))


def routed_local(
    output_grad,
    carried_grad,
    layer_inputs,
    expert_ids,
    gate_prob,
    gate_weight,
    up_weight,
    down_weight,
):
    expert_count = lax.axis_size("group") * lax.axis_size("local") // 2
    gate_local = gate_weight[0, 0]
    up_local = up_weight[0, 0]
    down_local = down_weight[0, 0]
    gate_other, up_other, down_other = swapped((gate_local, up_local, down_local), "local", 0)
    weights_local = (
        jnp.concatenate([gate_local, gate_other], axis=1),
        jnp.concatenate([up_local, up_other], axis=1),
        jnp.concatenate([down_local, down_other], axis=0),
    )
    last_section = lax.axis_index("pipe") == lax.axis_size("pipe") - 1
    micro_count = output_grad.shape[0]
    grads_out = []
    gates_out = []
    previous = carried_grad
    for micro_index in range(micro_count):
        if micro_index == 0:
            earlier = carried_grad
        else:
            earlier = from_behind(previous, "pipe", -1)
        incoming = jnp.where(last_section, output_grad[micro_index], earlier)
        result_grad, result_gate = layer_backward(
            incoming,
            layer_inputs[0, micro_index],
            expert_ids[0, micro_index],
            gate_prob[0, micro_index],
            weights_local,
            expert_count,
        )
        grads_out.append(result_grad)
        gates_out.append(result_gate)
        previous = result_grad
    return (jnp.stack(grads_out)[None], jnp.stack(gates_out)[None])


VMEM_LIMIT = 58 * 2**20
WIDTH_TILE = 512
LANES = 128


def tiles(total, step):
    return [(start, min(step, total - start)) for start in range(0, total, step)]


def whole_lanes(amount):
    return (amount + LANES - 1) // LANES * LANES


def begun(source, target, sem):
    copy = pltpu.make_async_copy(source, target, sem)
    copy.start()
    return copy


def pieces_begun(piece_refs, plan, rows_ref, sems):
    return [
        begun(
            ref.at[pl.ds(begin, rows), pl.ds(0, rows_ref.shape[1])],
            rows_ref.at[pl.ds(place, rows)],
            sems.at[number],
        )
        for number, (ref, (begin, rows, place)) in enumerate(zip(piece_refs, plan))
    ]


def both_begun(gate_hbm, up_hbm, both_ref, sems):
    hidden = gate_hbm.shape[0]
    padded = both_ref.shape[0] // 2
    return [
        begun(gate_hbm, both_ref.at[pl.ds(0, hidden)], sems.at[0]),
        begun(up_hbm, both_ref.at[pl.ds(padded, hidden)], sems.at[1]),
    ]


def math_kernel(plan, grad_plan, blocks, expert_ref, *refs):
    count, grad_count = len(plan), len(grad_plan)
    row_refs, grad_refs = refs[:count], refs[count : count + grad_count]
    gate_hbm, up_hbm, down_hbm = refs[count + grad_count : count + grad_count + 3]
    refs = refs[count + grad_count + 3 :]
    out_refs, refs = refs[: len(blocks)], refs[len(blocks) :]
    rows_ref, grad_rows_ref, down_ref, both_ref, grads_ref = refs[:5]
    piece_sems, grad_sems, sems, both_sems = refs[5:]
    hidden, width = down_ref.shape
    padded = both_ref.shape[0] // 2
    copies = pieces_begun(row_refs, plan, rows_ref, piece_sems)
    copies += both_begun(gate_hbm, up_hbm, both_ref, both_sems)
    late_copies = pieces_begun(grad_refs, grad_plan, grad_rows_ref, grad_sems)
    late_copies.append(begun(down_hbm, down_ref, sems.at[0]))
    for start in (hidden, padded + hidden):
        both_ref[pl.ds(start, padded - hidden), :] = jnp.zeros(
            (padded - hidden, width), jnp.bfloat16
        )
        grads_ref[:, pl.ds(start, padded - hidden)] = jnp.zeros(
            (grads_ref.shape[0], padded - hidden), jnp.bfloat16
        )
    for copy in copies:
        copy.wait()
    pre = lax.dot_general(
        rows_ref[...], both_ref[...], CONTRACT_LAST, preferred_element_type=jnp.float32
    )
    gate_pre, up_pre = pre[:, :hidden], pre[:, padded : padded + hidden]
    for copy in late_copies:
        copy.wait()
    back_proj = lax.dot_general(
        grad_rows_ref[:, :width], down_ref[...], CONTRACT_LAST, preferred_element_type=jnp.float32
    )
    lanes = lax.broadcasted_iota(jnp.int32, (1, LANES), 1)
    mine = lanes == expert_ref[0]
    probs = jnp.sum(
        jnp.where(mine, grad_rows_ref[:, width:].astype(jnp.float32), 0.0), axis=1, keepdims=True
    )
    sigmoid_gate = jax.nn.sigmoid(gate_pre)
    activated = gate_pre * sigmoid_gate
    scaled = probs * back_proj
    grads_ref[:, :hidden] = (
        scaled * up_pre * sigmoid_gate * (1.0 + gate_pre * (1.0 - sigmoid_gate))
    ).astype(jnp.bfloat16)
    grads_ref[:, pl.ds(padded, hidden)] = (scaled * activated).astype(jnp.bfloat16)
    part = jnp.sum(activated * up_pre * back_proj, axis=1, keepdims=True)
    part = jnp.where(mine, part, 0.0).astype(jnp.bfloat16)
    for out_ref, (place, amount) in zip(out_refs, blocks):
        out_ref[:, width:] = part[place : place + amount]
    for start, size in tiles(width, WIDTH_TILE):
        columns = pl.ds(start, size)
        grads = jnp.dot(
            grads_ref[...], both_ref[:, columns], preferred_element_type=jnp.float32
        ).astype(jnp.bfloat16)
        for out_ref, (place, amount) in zip(out_refs, blocks):
            out_ref[:, columns] = grads[place : place + amount]


ANYWHERE = pl.BlockSpec(memory_space=pl.ANY)
IN_VMEM = pl.BlockSpec(memory_space=pltpu.VMEM)


def expert_math(rows_in, plan, grads_in, grad_plan, blocks, expert, weights):
    hidden, width = weights[0].shape
    rows = sum(amount for _, amount in blocks)
    outs = [jax.ShapeDtypeStruct((amount, width + LANES), jnp.bfloat16) for _, amount in blocks]
    return pl.pallas_call(
        functools.partial(math_kernel, plan, grad_plan, blocks),
        out_shape=tuple(outs),
        in_specs=[pl.BlockSpec(memory_space=pltpu.SMEM)]
        + [ANYWHERE] * (len(rows_in) + len(grads_in) + 3),
        out_specs=(IN_VMEM,) * len(outs),
        scratch_shapes=[
            pltpu.VMEM((rows, width), jnp.bfloat16),
            pltpu.VMEM((rows, width + LANES), jnp.bfloat16),
            pltpu.VMEM((hidden, width), jnp.bfloat16),
            pltpu.VMEM((2 * whole_lanes(hidden), width), jnp.bfloat16),
            pltpu.VMEM((rows, 2 * whole_lanes(hidden)), jnp.bfloat16),
            pltpu.SemaphoreType.DMA((len(rows_in),)),
            pltpu.SemaphoreType.DMA((len(grads_in),)),
            pltpu.SemaphoreType.DMA((1,)),
            pltpu.SemaphoreType.DMA((2,)),
        ],
        compiler_params=pltpu.CompilerParams(vmem_limit_bytes=VMEM_LIMIT),
        cost_estimate=pl.CostEstimate(
            flops=10 * rows * width * hidden,
            bytes_accessed=6 * width * hidden + 6 * rows * width,
            transcendentals=rows * hidden,
        ),
        name="expert_math",
    )(expert, *rows_in, *grads_in, *weights)


def toggled(value, axis, mask):
    pairs = [(source, source ^ mask) for source in range(lax.axis_size(axis))]
    return lax.ppermute(value, axis, pairs)


def spread(block):
    near = toggled(block, "local", 1)
    far = toggled(block, "local", 2)
    first = [toggled(block, "group", 1)]
    second = [toggled(block, "group", 2)]
    corner = toggled(far, "local", 1)
    first += [toggled(column, "group", 1) for column in (far, corner)]
    second += [toggled(column, "group", 2) for column in (far, corner)]
    first.insert(1, toggled(first[0], "local", 1))
    second.insert(1, toggled(second[0], "local", 1))
    half = block.shape[0] // 2
    low = [toggled(column[:half], "group", 2) for column in first]
    high = [toggled(column[half:], "group", 1) for column in second]
    return list(zip((block, near, far, corner), first, second, low, high))


def piece_plan(found, begin, rows):
    half = found[0][0].shape[0] // 2
    arrays, plan = [], []
    for level, (column, first, second, low, high) in enumerate(found):
        for slot, array in ((0, column), (1, first), (2, second)):
            arrays.append(array)
            plan.append((begin, rows, (4 * slot + level) * rows))
        place = (12 + level) * rows
        upto = min(half, begin + rows)
        if begin < upto:
            arrays.append(low)
            plan.append((begin, upto - begin, place))
        since = max(half, begin)
        if since < begin + rows:
            arrays.append(high)
            plan.append((since - half, begin + rows - since, place + since - begin))
    return arrays, tuple(plan)


def added(*values):
    total = values[0].astype(jnp.float32)
    for value in values[1:]:
        total = total + value.astype(jnp.float32)
    return total


def result_blocks(rows):
    quarter = 4 * rows
    diag = [(3 * quarter + level * rows, rows) for level in range(4)]
    sides = []
    for start in (quarter, 2 * quarter):
        sides += [(start + level * rows, rows) for level in range(4)]
    own = [(0, 2 * rows), (2 * rows, rows), (3 * rows, rows)]
    return tuple(diag + sides + own)


def narrowed(value):
    return value.astype(jnp.bfloat16)


def brought_back(blocks):
    diag_0, diag_1, diag_2, diag_3 = blocks[:4]
    first_0, first_1, first_2, first_3, second_0, second_1, second_2, second_3 = blocks[4:12]
    own_low, own_2, own_3 = blocks[12:]
    rows = diag_0.shape[0]
    got_2 = toggled(diag_2, "group", 1)
    got_3 = toggled(diag_3, "group", 2)
    got_0 = toggled(diag_0, "group", 1)
    got_1 = toggled(diag_1, "group", 2)
    from_first_2 = toggled(first_2, "group", 1)
    from_second_3 = toggled(second_3, "group", 2)
    from_first_3 = toggled(narrowed(added(first_3, got_3)), "group", 1)
    from_second_2 = toggled(narrowed(added(second_2, got_2)), "group", 2)
    from_far = toggled(narrowed(added(own_2, from_first_2, from_second_2)), "local", 2)
    from_corner = toggled(narrowed(added(own_3, from_first_3, from_second_3)), "local", 3)
    first_low = jnp.concatenate([first_0, narrowed(added(first_1, got_1))])
    second_low = jnp.concatenate([narrowed(added(second_0, got_0)), second_1])
    from_first_low = toggled(first_low, "group", 1)
    from_second_low = toggled(second_low, "group", 2)
    low = added(own_low, from_first_low, from_second_low)
    from_near = toggled(narrowed(low[rows:]), "local", 1)
    return added(low[:rows], from_near, from_far, from_corner)


def dense_local(
    output_grad,
    carried_grad,
    layer_inputs,
    expert_ids,
    gate_prob,
    gate_weight,
    up_weight,
    down_weight,
):
    expert_count = lax.axis_size("group") * lax.axis_size("local") // 2
    micro_count, rows, width = output_grad.shape
    gate_half, up_half, down_half = gate_weight[0, 0].T, up_weight[0, 0].T, down_weight[0, 0]
    own_index = lax.axis_index("group") * lax.axis_size("local") + lax.axis_index("local")
    expert = jnp.reshape(own_index // 2, (1,)).astype(jnp.int32)
    matches = (expert_ids[0][..., None] == jnp.arange(LANES, dtype=jnp.int32)).astype(jnp.float32)
    token_probs = jnp.sum(matches * gate_prob[0].astype(jnp.float32)[..., None], axis=2)
    token_probs = token_probs.astype(jnp.bfloat16)
    last_section = lax.axis_index("pipe") == lax.axis_size("pipe") - 1
    inputs = layer_inputs[0]
    blocks = result_blocks(rows)
    weights = (gate_half, up_half, down_half)
    none = jnp.zeros((rows, LANES), jnp.bfloat16)
    earlier = carried_grad
    grads_out, gates = [], []
    for m in range(micro_count):
        if m > 0:
            earlier = from_behind(grads_out[-1], "pipe", -1)
        incoming = jnp.where(last_section, output_grad[m], earlier)
        sent = jnp.concatenate(
            [
                jnp.concatenate([inputs[m], incoming], axis=0),
                jnp.concatenate([none, token_probs[m]], axis=0),
            ],
            axis=1,
        )
        found = spread(sent)
        arrays, plan = piece_plan(found, 0, rows)
        grad_arrays, grad_plan = piece_plan(found, rows, rows)
        pieces = expert_math(arrays, plan, grad_arrays, grad_plan, blocks, expert, weights)
        total = brought_back(pieces)
        grads_out.append(added(incoming, total[:, :width]).astype(jnp.bfloat16))
        gates.append(total[:, width:])
    gates = jnp.sum(matches * jnp.stack(gates)[:, :, None, :], axis=3).astype(jnp.bfloat16)
    return (jnp.stack(grads_out)[None], gates[None])


def local(*arguments):
    group, ring = lax.axis_size("group"), lax.axis_size("local")
    top_count = arguments[3].shape[-1]
    expert_count = group * ring // 2
    crowded = 3 * expert_count <= 4 * top_count
    if group == 4 and ring == 4 and crowded and expert_count <= LANES:
        return dense_local(*arguments)
    return routed_local(*arguments)


def solution(mesh):
    return jax.shard_map(
        local,
        mesh=mesh,
        in_specs=(
            P(None, ("group", "local"), None),
            P(("group", "local"), None),
            P("pipe", None, ("group", "local"), None),
            P("pipe", None, ("group", "local"), None),
            P("pipe", None, ("group", "local"), None),
            P("pipe", ("group", "local"), None, None),
            P("pipe", ("group", "local"), None, None),
            P("pipe", ("group", "local"), None, None),
        ),
        out_specs=(
            P("pipe", None, ("group", "local"), None),
            P("pipe", None, ("group", "local"), None),
        ),
        check_vma=False,
    )
```

```python
import functools

import jax
import jax.numpy as jnp
from jax import lax
from jax.experimental import pallas as pl
from jax.experimental.pallas import tpu as pltpu
from jax.sharding import PartitionSpec as P

CONTRACT_LAST = (((1,), (1,)), ((), ()))
CONTRACT_FIRST = (((0,), (0,)), ((), ()))


def swapped(value, axis, bit):
    mask = 2**bit
    pairs = [(source, source ^ mask) for source in range(lax.axis_size(axis))]
    return lax.ppermute(value, axis, pairs)


def from_behind(block, axis, distance):
    devices = range(lax.axis_size(axis))
    route = [(i - distance, i) for i in devices if i - distance in devices]
    return lax.ppermute(block, axis, route)


def expert_backward(rows_in, rows_grad, row_probs, gate_full, up_full, down_full):
    gate_pre = jnp.dot(rows_in, gate_full, preferred_element_type=jnp.float32)
    up_pre = jnp.dot(rows_in, up_full, preferred_element_type=jnp.float32)
    back_proj = lax.dot_general(
        rows_grad, down_full, CONTRACT_LAST, preferred_element_type=jnp.float32
    )
    sigmoid_gate = jax.nn.sigmoid(gate_pre)
    activated = gate_pre * sigmoid_gate
    gate_part = jnp.sum(activated * up_pre * back_proj, axis=1)
    scaled = row_probs.astype(jnp.float32)[:, None] * back_proj
    grad_gate = (scaled * up_pre * sigmoid_gate * (1.0 + gate_pre * (1.0 - sigmoid_gate))).astype(
        jnp.bfloat16
    )
    grad_up = (scaled * activated).astype(jnp.bfloat16)
    grad_rows = lax.dot_general(
        grad_gate, gate_full, CONTRACT_LAST, preferred_element_type=jnp.float32
    )
    grad_rows = grad_rows + lax.dot_general(
        grad_up, up_full, CONTRACT_LAST, preferred_element_type=jnp.float32
    )
    return (grad_rows, gate_part)


def route_tables(choice_ids, choice_probs, expert_count, capacity):
    expert_range = jnp.arange(expert_count, dtype=jnp.int32)
    matches = (choice_ids[:, :, None] == expert_range[None, None, :]).astype(jnp.int32)
    chosen = jnp.sum(matches, axis=1)
    rows = jnp.arange(choice_ids.shape[0])
    earlier = (rows[:, None] > rows[None, :]).astype(jnp.float32)
    before = jnp.dot(earlier, chosen.astype(jnp.float32)).astype(jnp.int32)
    slot_range = jnp.arange(capacity, dtype=jnp.int32)
    placed = (before[:, :, None] == slot_range[None, None, :]) & (chosen[:, :, None] > 0)
    slot_map = jnp.transpose(placed, (1, 2, 0)).astype(jnp.float32)
    token_probs = jnp.sum(
        matches.astype(jnp.float32) * choice_probs.astype(jnp.float32)[:, :, None], axis=1
    )
    slot_probs = jnp.einsum("ect,te->ec", slot_map, token_probs)
    return (matches, slot_map, slot_probs)


def layer_backward(incoming, inputs, choice_ids, choice_probs, weights_local, expert_count):
    tokens_here = incoming.shape[0]
    model_width = incoming.shape[1]
    top_count = choice_ids.shape[1]
    capacity = 2 * ((tokens_here * top_count * 2 + 3 * expert_count - 1) // (3 * expert_count))
    half_slots = capacity // 2
    devices = 2 * expert_count
    matches, slot_map, slot_probs = route_tables(choice_ids, choice_probs, expert_count, capacity)
    flat_map = slot_map.reshape(expert_count * capacity, tokens_here).astype(jnp.bfloat16)
    sent_inputs = jnp.dot(flat_map, inputs, preferred_element_type=jnp.float32).astype(jnp.bfloat16)
    sent_grads = jnp.dot(flat_map, incoming, preferred_element_type=jnp.float32).astype(
        jnp.bfloat16
    )
    sent_probs = slot_probs.reshape(expert_count * capacity).astype(jnp.bfloat16)
    gate_full, up_full, down_full = weights_local
    got_inputs, got_grads, got_probs = (
        lax.all_to_all(sent_inputs, ("group", "local"), split_axis=0, concat_axis=0, tiled=True),
        lax.all_to_all(sent_grads, ("group", "local"), split_axis=0, concat_axis=0, tiled=True),
        lax.all_to_all(sent_probs, ("group", "local"), split_axis=0, concat_axis=0, tiled=True),
    )
    grad_rows, gate_part = expert_backward(
        got_inputs, got_grads, got_probs, gate_full, up_full, down_full
    )
    kept_grad = grad_rows.reshape(devices, half_slots, model_width)
    kept_part = gate_part.reshape(devices, half_slots)
    back_grad, back_part = (
        lax.all_to_all(
            kept_grad.astype(jnp.bfloat16),
            ("group", "local"),
            split_axis=0,
            concat_axis=0,
            tiled=True,
        ),
        lax.all_to_all(
            kept_part.astype(jnp.bfloat16),
            ("group", "local"),
            split_axis=0,
            concat_axis=0,
            tiled=True,
        ),
    )
    back_grad = back_grad.reshape(expert_count * capacity, model_width)
    summed = incoming.astype(jnp.float32) + lax.dot_general(
        flat_map, back_grad, CONTRACT_FIRST, preferred_element_type=jnp.float32
    )
    per_expert = jnp.einsum(
        "ect,ec->te", slot_map, back_part.reshape(expert_count, capacity).astype(jnp.float32)
    )
    gate_values = jnp.sum(matches.astype(jnp.float32) * per_expert[:, None, :], axis=2)
    return (summed.astype(jnp.bfloat16), gate_values.astype(jnp.bfloat16))


def routed_local(
    output_grad,
    carried_grad,
    layer_inputs,
    expert_ids,
    gate_prob,
    gate_weight,
    up_weight,
    down_weight,
):
    expert_count = lax.axis_size("group") * lax.axis_size("local") // 2
    gate_local = gate_weight[0, 0]
    up_local = up_weight[0, 0]
    down_local = down_weight[0, 0]
    gate_other, up_other, down_other = swapped((gate_local, up_local, down_local), "local", 0)
    weights_local = (
        jnp.concatenate([gate_local, gate_other], axis=1),
        jnp.concatenate([up_local, up_other], axis=1),
        jnp.concatenate([down_local, down_other], axis=0),
    )
    last_section = lax.axis_index("pipe") == lax.axis_size("pipe") - 1
    micro_count = output_grad.shape[0]
    grads_out = []
    gates_out = []
    previous = carried_grad
    for micro_index in range(micro_count):
        if micro_index == 0:
            earlier = carried_grad
        else:
            earlier = from_behind(previous, "pipe", -1)
        incoming = jnp.where(last_section, output_grad[micro_index], earlier)
        result_grad, result_gate = layer_backward(
            incoming,
            layer_inputs[0, micro_index],
            expert_ids[0, micro_index],
            gate_prob[0, micro_index],
            weights_local,
            expert_count,
        )
        grads_out.append(result_grad)
        gates_out.append(result_gate)
        previous = result_grad
    return (jnp.stack(grads_out)[None], jnp.stack(gates_out)[None])


VMEM_LIMIT = 50 * 2**20
WIDTH_TILE = 512
LANES = 128


def tiles(total, step):
    return [(start, min(step, total - start)) for start in range(0, total, step)]


def whole_lanes(amount):
    return (amount + LANES - 1) // LANES * LANES


def begun(source, target, sem):
    copy = pltpu.make_async_copy(source, target, sem)
    copy.start()
    return copy


def pieces_begun(piece_refs, plan, rows_ref, sems):
    return [
        begun(
            ref.at[pl.ds(begin, rows), pl.ds(0, rows_ref.shape[1])],
            rows_ref.at[pl.ds(place, rows)],
            sems.at[number],
        )
        for number, (ref, (begin, rows, place)) in enumerate(zip(piece_refs, plan))
    ]


def both_begun(gate_hbm, up_hbm, both_ref, sems):
    hidden = gate_hbm.shape[0]
    padded = both_ref.shape[0] // 2
    return [
        begun(gate_hbm, both_ref.at[pl.ds(0, hidden)], sems.at[0]),
        begun(up_hbm, both_ref.at[pl.ds(padded, hidden)], sems.at[1]),
    ]


def math_kernel(plan, grad_plan, blocks, expert_ref, *refs):
    count, grad_count = len(plan), len(grad_plan)
    row_refs, grad_refs = refs[:count], refs[count : count + grad_count]
    gate_hbm, up_hbm, down_hbm = refs[count + grad_count : count + grad_count + 3]
    refs = refs[count + grad_count + 3 :]
    out_refs, refs = refs[: len(blocks)], refs[len(blocks) :]
    rows_ref, grad_rows_ref, down_ref, both_ref, grads_ref = refs[:5]
    piece_sems, grad_sems, sems, both_sems = refs[5:]
    hidden, width = down_ref.shape
    padded = both_ref.shape[0] // 2
    copies = pieces_begun(row_refs, plan, rows_ref, piece_sems)
    copies += both_begun(gate_hbm, up_hbm, both_ref, both_sems)
    late_copies = pieces_begun(grad_refs, grad_plan, grad_rows_ref, grad_sems)
    late_copies.append(begun(down_hbm, down_ref, sems.at[0]))
    for start in (hidden, padded + hidden):
        both_ref[pl.ds(start, padded - hidden), :] = jnp.zeros(
            (padded - hidden, width), jnp.bfloat16
        )
        grads_ref[:, pl.ds(start, padded - hidden)] = jnp.zeros(
            (grads_ref.shape[0], padded - hidden), jnp.bfloat16
        )
    for copy in copies:
        copy.wait()
    pre = lax.dot_general(
        rows_ref[...], both_ref[...], CONTRACT_LAST, preferred_element_type=jnp.float32
    )
    gate_pre, up_pre = pre[:, :hidden], pre[:, padded : padded + hidden]
    for copy in late_copies:
        copy.wait()
    back_proj = lax.dot_general(
        grad_rows_ref[:, :width], down_ref[...], CONTRACT_LAST, preferred_element_type=jnp.float32
    )
    lanes = lax.broadcasted_iota(jnp.int32, (1, LANES), 1)
    mine = lanes == expert_ref[0]
    probs = jnp.sum(
        jnp.where(mine, grad_rows_ref[:, width:].astype(jnp.float32), 0.0), axis=1, keepdims=True
    )
    sigmoid_gate = jax.nn.sigmoid(gate_pre)
    activated = gate_pre * sigmoid_gate
    scaled = probs * back_proj
    grads_ref[:, :hidden] = (
        scaled * up_pre * sigmoid_gate * (1.0 + gate_pre * (1.0 - sigmoid_gate))
    ).astype(jnp.bfloat16)
    grads_ref[:, pl.ds(padded, hidden)] = (scaled * activated).astype(jnp.bfloat16)
    part = jnp.sum(activated * up_pre * back_proj, axis=1, keepdims=True)
    part = jnp.where(mine, part, 0.0).astype(jnp.bfloat16)
    for out_ref, (place, amount) in zip(out_refs, blocks):
        out_ref[:, width:] = part[place : place + amount]
    for start, size in tiles(width, WIDTH_TILE):
        columns = pl.ds(start, size)
        grads = jnp.dot(
            grads_ref[...], both_ref[:, columns], preferred_element_type=jnp.float32
        ).astype(jnp.bfloat16)
        for out_ref, (place, amount) in zip(out_refs, blocks):
            out_ref[:, columns] = grads[place : place + amount]


ANYWHERE = pl.BlockSpec(memory_space=pl.ANY)
IN_VMEM = pl.BlockSpec(memory_space=pltpu.VMEM)


def expert_math(rows_in, plan, grads_in, grad_plan, blocks, expert, weights):
    hidden, width = weights[0].shape
    rows = sum(amount for _, amount in blocks)
    outs = [jax.ShapeDtypeStruct((amount, width + LANES), jnp.bfloat16) for _, amount in blocks]
    return pl.pallas_call(
        functools.partial(math_kernel, plan, grad_plan, blocks),
        out_shape=tuple(outs),
        in_specs=[pl.BlockSpec(memory_space=pltpu.SMEM)]
        + [ANYWHERE] * (len(rows_in) + len(grads_in) + 3),
        out_specs=(IN_VMEM,) * len(outs),
        scratch_shapes=[
            pltpu.VMEM((rows, width), jnp.bfloat16),
            pltpu.VMEM((rows, width + LANES), jnp.bfloat16),
            pltpu.VMEM((hidden, width), jnp.bfloat16),
            pltpu.VMEM((2 * whole_lanes(hidden), width), jnp.bfloat16),
            pltpu.VMEM((rows, 2 * whole_lanes(hidden)), jnp.bfloat16),
            pltpu.SemaphoreType.DMA((len(rows_in),)),
            pltpu.SemaphoreType.DMA((len(grads_in),)),
            pltpu.SemaphoreType.DMA((1,)),
            pltpu.SemaphoreType.DMA((2,)),
        ],
        compiler_params=pltpu.CompilerParams(vmem_limit_bytes=VMEM_LIMIT),
        cost_estimate=pl.CostEstimate(
            flops=10 * rows * width * hidden,
            bytes_accessed=6 * width * hidden + 6 * rows * width,
            transcendentals=rows * hidden,
        ),
        name="expert_math",
    )(expert, *rows_in, *grads_in, *weights)


def toggled(value, axis, mask):
    pairs = [(source, source ^ mask) for source in range(lax.axis_size(axis))]
    return lax.ppermute(value, axis, pairs)


def spread(block):
    near = toggled(block, "local", 1)
    far = toggled(block, "local", 2)
    first = [toggled(block, "group", 1)]
    second = [toggled(block, "group", 2)]
    corner = toggled(far, "local", 1)
    first += [toggled(column, "group", 1) for column in (far, corner)]
    second += [toggled(column, "group", 2) for column in (far, corner)]
    first.insert(1, toggled(first[0], "local", 1))
    second.insert(1, toggled(second[0], "local", 1))
    half = block.shape[0] // 2
    low = [toggled(column[:half], "group", 2) for column in first]
    high = [toggled(column[half:], "group", 1) for column in second]
    return list(zip((block, near, far, corner), first, second, low, high))


def piece_plan(found, begin, rows):
    half = found[0][0].shape[0] // 2
    arrays, plan = [], []
    for level, (column, first, second, low, high) in enumerate(found):
        for slot, array in ((0, column), (1, first), (2, second)):
            arrays.append(array)
            plan.append((begin, rows, (4 * slot + level) * rows))
        place = (12 + level) * rows
        upto = min(half, begin + rows)
        if begin < upto:
            arrays.append(low)
            plan.append((begin, upto - begin, place))
        since = max(half, begin)
        if since < begin + rows:
            arrays.append(high)
            plan.append((since - half, begin + rows - since, place + since - begin))
    return arrays, tuple(plan)


def added(*values):
    total = values[0].astype(jnp.float32)
    for value in values[1:]:
        total = total + value.astype(jnp.float32)
    return total


def result_blocks(rows):
    quarter = 4 * rows
    diag = [(3 * quarter + level * rows, rows) for level in range(4)]
    sides = []
    for start in (quarter, 2 * quarter):
        sides += [(start + level * rows, rows) for level in range(4)]
    own = [(0, 2 * rows), (2 * rows, rows), (3 * rows, rows)]
    return tuple(diag + sides + own)


def narrowed(value):
    return value.astype(jnp.bfloat16)


def brought_back(blocks):
    diag_0, diag_1, diag_2, diag_3 = blocks[:4]
    first_0, first_1, first_2, first_3, second_0, second_1, second_2, second_3 = blocks[4:12]
    own_low, own_2, own_3 = blocks[12:]
    rows = diag_0.shape[0]
    got_2 = toggled(diag_2, "group", 1)
    got_3 = toggled(diag_3, "group", 2)
    got_0 = toggled(diag_0, "group", 1)
    got_1 = toggled(diag_1, "group", 2)
    from_first_2 = toggled(first_2, "group", 1)
    from_second_3 = toggled(second_3, "group", 2)
    from_first_3 = toggled(narrowed(added(first_3, got_3)), "group", 1)
    from_second_2 = toggled(narrowed(added(second_2, got_2)), "group", 2)
    from_far = toggled(narrowed(added(own_2, from_first_2, from_second_2)), "local", 2)
    from_corner = toggled(narrowed(added(own_3, from_first_3, from_second_3)), "local", 3)
    first_low = jnp.concatenate([first_0, narrowed(added(first_1, got_1))])
    second_low = jnp.concatenate([narrowed(added(second_0, got_0)), second_1])
    from_first_low = toggled(first_low, "group", 1)
    from_second_low = toggled(second_low, "group", 2)
    low = added(own_low, from_first_low, from_second_low)
    from_near = toggled(narrowed(low[rows:]), "local", 1)
    return added(low[:rows], from_near, from_far, from_corner)


def dense_local(
    output_grad,
    carried_grad,
    layer_inputs,
    expert_ids,
    gate_prob,
    gate_weight,
    up_weight,
    down_weight,
):
    expert_count = lax.axis_size("group") * lax.axis_size("local") // 2
    micro_count, rows, width = output_grad.shape
    gate_half, up_half, down_half = gate_weight[0, 0].T, up_weight[0, 0].T, down_weight[0, 0]
    own_index = lax.axis_index("group") * lax.axis_size("local") + lax.axis_index("local")
    expert = jnp.reshape(own_index // 2, (1,)).astype(jnp.int32)
    matches = (expert_ids[0][..., None] == jnp.arange(LANES, dtype=jnp.int32)).astype(jnp.float32)
    token_probs = jnp.sum(matches * gate_prob[0].astype(jnp.float32)[..., None], axis=2)
    token_probs = token_probs.astype(jnp.bfloat16)
    last_section = lax.axis_index("pipe") == lax.axis_size("pipe") - 1
    inputs = layer_inputs[0]
    blocks = result_blocks(rows)
    weights = (gate_half, up_half, down_half)
    none = jnp.zeros((rows, LANES), jnp.bfloat16)
    earlier = carried_grad
    grads_out, gates = [], []
    for m in range(micro_count):
        if m > 0:
            earlier = from_behind(grads_out[-1], "pipe", -1)
        incoming = jnp.where(last_section, output_grad[m], earlier)
        sent = jnp.concatenate(
            [
                jnp.concatenate([inputs[m], incoming], axis=0),
                jnp.concatenate([none, token_probs[m]], axis=0),
            ],
            axis=1,
        )
        found = spread(sent)
        arrays, plan = piece_plan(found, 0, rows)
        grad_arrays, grad_plan = piece_plan(found, rows, rows)
        pieces = expert_math(arrays, plan, grad_arrays, grad_plan, blocks, expert, weights)
        total = brought_back(pieces)
        grads_out.append(added(incoming, total[:, :width]).astype(jnp.bfloat16))
        gates.append(total[:, width:])
    gates = jnp.sum(matches * jnp.stack(gates)[:, :, None, :], axis=3).astype(jnp.bfloat16)
    return (jnp.stack(grads_out)[None], gates[None])


def local(*arguments):
    group, ring = lax.axis_size("group"), lax.axis_size("local")
    top_count = arguments[3].shape[-1]
    expert_count = group * ring // 2
    crowded = 3 * expert_count <= 4 * top_count
    if group == 4 and ring == 4 and crowded and expert_count <= LANES:
        return dense_local(*arguments)
    return routed_local(*arguments)


def solution(mesh):
    return jax.shard_map(
        local,
        mesh=mesh,
        in_specs=(
            P(None, ("group", "local"), None),
            P(("group", "local"), None),
            P("pipe", None, ("group", "local"), None),
            P("pipe", None, ("group", "local"), None),
            P("pipe", None, ("group", "local"), None),
            P("pipe", ("group", "local"), None, None),
            P("pipe", ("group", "local"), None, None),
            P("pipe", ("group", "local"), None, None),
        ),
        out_specs=(
            P("pipe", None, ("group", "local"), None),
            P("pipe", None, ("group", "local"), None),
        ),
        check_vma=False,
    )
```

```python
import functools

import jax
import jax.numpy as jnp
from jax import lax
from jax.experimental import pallas as pl
from jax.experimental.pallas import tpu as pltpu
from jax.sharding import PartitionSpec as P

CONTRACT_LAST = (((1,), (1,)), ((), ()))
CONTRACT_FIRST = (((0,), (0,)), ((), ()))


def swapped(value, axis, bit):
    mask = 2**bit
    pairs = [(source, source ^ mask) for source in range(lax.axis_size(axis))]
    return lax.ppermute(value, axis, pairs)


def from_behind(block, axis, distance):
    devices = range(lax.axis_size(axis))
    route = [(i - distance, i) for i in devices if i - distance in devices]
    return lax.ppermute(block, axis, route)


def expert_backward(rows_in, rows_grad, row_probs, gate_full, up_full, down_full):
    gate_pre = jnp.dot(rows_in, gate_full, preferred_element_type=jnp.float32)
    up_pre = jnp.dot(rows_in, up_full, preferred_element_type=jnp.float32)
    back_proj = lax.dot_general(
        rows_grad, down_full, CONTRACT_LAST, preferred_element_type=jnp.float32
    )
    sigmoid_gate = jax.nn.sigmoid(gate_pre)
    activated = gate_pre * sigmoid_gate
    gate_part = jnp.sum(activated * up_pre * back_proj, axis=1)
    scaled = row_probs.astype(jnp.float32)[:, None] * back_proj
    grad_gate = (scaled * up_pre * sigmoid_gate * (1.0 + gate_pre * (1.0 - sigmoid_gate))).astype(
        jnp.bfloat16
    )
    grad_up = (scaled * activated).astype(jnp.bfloat16)
    grad_rows = lax.dot_general(
        grad_gate, gate_full, CONTRACT_LAST, preferred_element_type=jnp.float32
    )
    grad_rows = grad_rows + lax.dot_general(
        grad_up, up_full, CONTRACT_LAST, preferred_element_type=jnp.float32
    )
    return (grad_rows, gate_part)


def route_tables(choice_ids, choice_probs, expert_count, capacity):
    expert_range = jnp.arange(expert_count, dtype=jnp.int32)
    matches = (choice_ids[:, :, None] == expert_range[None, None, :]).astype(jnp.int32)
    chosen = jnp.sum(matches, axis=1)
    rows = jnp.arange(choice_ids.shape[0])
    earlier = (rows[:, None] > rows[None, :]).astype(jnp.float32)
    before = jnp.dot(earlier, chosen.astype(jnp.float32)).astype(jnp.int32)
    slot_range = jnp.arange(capacity, dtype=jnp.int32)
    placed = (before[:, :, None] == slot_range[None, None, :]) & (chosen[:, :, None] > 0)
    slot_map = jnp.transpose(placed, (1, 2, 0)).astype(jnp.float32)
    token_probs = jnp.sum(
        matches.astype(jnp.float32) * choice_probs.astype(jnp.float32)[:, :, None], axis=1
    )
    slot_probs = jnp.einsum("ect,te->ec", slot_map, token_probs)
    return (matches, slot_map, slot_probs)


def layer_backward(incoming, inputs, choice_ids, choice_probs, weights_local, expert_count):
    tokens_here = incoming.shape[0]
    model_width = incoming.shape[1]
    top_count = choice_ids.shape[1]
    capacity = 2 * ((tokens_here * top_count * 2 + 3 * expert_count - 1) // (3 * expert_count))
    half_slots = capacity // 2
    devices = 2 * expert_count
    matches, slot_map, slot_probs = route_tables(choice_ids, choice_probs, expert_count, capacity)
    flat_map = slot_map.reshape(expert_count * capacity, tokens_here).astype(jnp.bfloat16)
    sent_inputs = jnp.dot(flat_map, inputs, preferred_element_type=jnp.float32).astype(jnp.bfloat16)
    sent_grads = jnp.dot(flat_map, incoming, preferred_element_type=jnp.float32).astype(
        jnp.bfloat16
    )
    sent_probs = slot_probs.reshape(expert_count * capacity).astype(jnp.bfloat16)
    gate_full, up_full, down_full = weights_local
    got_inputs, got_grads, got_probs = (
        lax.all_to_all(sent_inputs, ("group", "local"), split_axis=0, concat_axis=0, tiled=True),
        lax.all_to_all(sent_grads, ("group", "local"), split_axis=0, concat_axis=0, tiled=True),
        lax.all_to_all(sent_probs, ("group", "local"), split_axis=0, concat_axis=0, tiled=True),
    )
    grad_rows, gate_part = expert_backward(
        got_inputs, got_grads, got_probs, gate_full, up_full, down_full
    )
    kept_grad = grad_rows.reshape(devices, half_slots, model_width)
    kept_part = gate_part.reshape(devices, half_slots)
    back_grad, back_part = (
        lax.all_to_all(
            kept_grad.astype(jnp.bfloat16),
            ("group", "local"),
            split_axis=0,
            concat_axis=0,
            tiled=True,
        ),
        lax.all_to_all(
            kept_part.astype(jnp.bfloat16),
            ("group", "local"),
            split_axis=0,
            concat_axis=0,
            tiled=True,
        ),
    )
    back_grad = back_grad.reshape(expert_count * capacity, model_width)
    summed = incoming.astype(jnp.float32) + lax.dot_general(
        flat_map, back_grad, CONTRACT_FIRST, preferred_element_type=jnp.float32
    )
    per_expert = jnp.einsum(
        "ect,ec->te", slot_map, back_part.reshape(expert_count, capacity).astype(jnp.float32)
    )
    gate_values = jnp.sum(matches.astype(jnp.float32) * per_expert[:, None, :], axis=2)
    return (summed.astype(jnp.bfloat16), gate_values.astype(jnp.bfloat16))


def routed_local(
    output_grad,
    carried_grad,
    layer_inputs,
    expert_ids,
    gate_prob,
    gate_weight,
    up_weight,
    down_weight,
):
    expert_count = lax.axis_size("group") * lax.axis_size("local") // 2
    gate_local = gate_weight[0, 0]
    up_local = up_weight[0, 0]
    down_local = down_weight[0, 0]
    gate_other, up_other, down_other = swapped((gate_local, up_local, down_local), "local", 0)
    weights_local = (
        jnp.concatenate([gate_local, gate_other], axis=1),
        jnp.concatenate([up_local, up_other], axis=1),
        jnp.concatenate([down_local, down_other], axis=0),
    )
    last_section = lax.axis_index("pipe") == lax.axis_size("pipe") - 1
    micro_count = output_grad.shape[0]
    grads_out = []
    gates_out = []
    previous = carried_grad
    for micro_index in range(micro_count):
        if micro_index == 0:
            earlier = carried_grad
        else:
            earlier = from_behind(previous, "pipe", -1)
        incoming = jnp.where(last_section, output_grad[micro_index], earlier)
        result_grad, result_gate = layer_backward(
            incoming,
            layer_inputs[0, micro_index],
            expert_ids[0, micro_index],
            gate_prob[0, micro_index],
            weights_local,
            expert_count,
        )
        grads_out.append(result_grad)
        gates_out.append(result_gate)
        previous = result_grad
    return (jnp.stack(grads_out)[None], jnp.stack(gates_out)[None])


VMEM_LIMIT = 50 * 2**20
WIDTH_TILE = 512
LANES = 128


def tiles(total, step):
    return [(start, min(step, total - start)) for start in range(0, total, step)]


def whole_lanes(amount):
    return (amount + LANES - 1) // LANES * LANES


def begun(source, target, sem):
    copy = pltpu.make_async_copy(source, target, sem)
    copy.start()
    return copy


def pieces_begun(piece_refs, plan, rows_ref, sems):
    return [
        begun(
            ref.at[pl.ds(begin, rows), pl.ds(0, rows_ref.shape[1])],
            rows_ref.at[pl.ds(place, rows)],
            sems.at[number],
        )
        for number, (ref, (begin, rows, place)) in enumerate(zip(piece_refs, plan))
    ]


def both_begun(gate_hbm, up_hbm, both_ref, sems):
    hidden = gate_hbm.shape[0]
    padded = both_ref.shape[0] // 2
    return [
        begun(gate_hbm, both_ref.at[pl.ds(0, hidden)], sems.at[0]),
        begun(up_hbm, both_ref.at[pl.ds(padded, hidden)], sems.at[1]),
    ]


def math_kernel(plan, grad_plan, blocks, expert_ref, *refs):
    count, grad_count = len(plan), len(grad_plan)
    row_refs, grad_refs = refs[:count], refs[count : count + grad_count]
    gate_hbm, up_hbm, down_hbm = refs[count + grad_count : count + grad_count + 3]
    refs = refs[count + grad_count + 3 :]
    out_refs, refs = refs[: len(blocks)], refs[len(blocks) :]
    rows_ref, grad_rows_ref, down_ref, both_ref, grads_ref = refs[:5]
    piece_sems, grad_sems, sems, both_sems = refs[5:]
    hidden, width = down_ref.shape
    padded = both_ref.shape[0] // 2
    copies = pieces_begun(row_refs, plan, rows_ref, piece_sems)
    copies += both_begun(gate_hbm, up_hbm, both_ref, both_sems)
    late_copies = pieces_begun(grad_refs, grad_plan, grad_rows_ref, grad_sems)
    late_copies.append(begun(down_hbm, down_ref, sems.at[0]))
    for start in (hidden, padded + hidden):
        both_ref[pl.ds(start, padded - hidden), :] = jnp.zeros(
            (padded - hidden, width), jnp.bfloat16
        )
        grads_ref[:, pl.ds(start, padded - hidden)] = jnp.zeros(
            (grads_ref.shape[0], padded - hidden), jnp.bfloat16
        )
    for copy in copies:
        copy.wait()
    pre = lax.dot_general(
        rows_ref[...], both_ref[...], CONTRACT_LAST, preferred_element_type=jnp.float32
    )
    gate_pre, up_pre = pre[:, :hidden], pre[:, padded : padded + hidden]
    for copy in late_copies:
        copy.wait()
    back_proj = lax.dot_general(
        grad_rows_ref[:, :width], down_ref[...], CONTRACT_LAST, preferred_element_type=jnp.float32
    )
    lanes = lax.broadcasted_iota(jnp.int32, (1, LANES), 1)
    mine = lanes == expert_ref[0]
    probs = jnp.sum(
        jnp.where(mine, grad_rows_ref[:, width:].astype(jnp.float32), 0.0), axis=1, keepdims=True
    )
    sigmoid_gate = jax.nn.sigmoid(gate_pre)
    activated = gate_pre * sigmoid_gate
    scaled = probs * back_proj
    grads_ref[:, :hidden] = (
        scaled * up_pre * sigmoid_gate * (1.0 + gate_pre * (1.0 - sigmoid_gate))
    ).astype(jnp.bfloat16)
    grads_ref[:, pl.ds(padded, hidden)] = (scaled * activated).astype(jnp.bfloat16)
    part = jnp.sum(activated * up_pre * back_proj, axis=1, keepdims=True)
    part = jnp.where(mine, part, 0.0).astype(jnp.bfloat16)
    for out_ref, (place, amount) in zip(out_refs, blocks):
        out_ref[:, width:] = part[place : place + amount]
    for start, size in tiles(width, WIDTH_TILE):
        columns = pl.ds(start, size)
        grads = jnp.dot(
            grads_ref[...], both_ref[:, columns], preferred_element_type=jnp.float32
        ).astype(jnp.bfloat16)
        for out_ref, (place, amount) in zip(out_refs, blocks):
            out_ref[:, columns] = grads[place : place + amount]


ANYWHERE = pl.BlockSpec(memory_space=pl.ANY)
IN_VMEM = pl.BlockSpec(memory_space=pltpu.VMEM)


def expert_math(rows_in, plan, grads_in, grad_plan, blocks, expert, weights):
    hidden, width = weights[0].shape
    rows = sum(amount for _, amount in blocks)
    outs = [jax.ShapeDtypeStruct((amount, width + LANES), jnp.bfloat16) for _, amount in blocks]
    return pl.pallas_call(
        functools.partial(math_kernel, plan, grad_plan, blocks),
        out_shape=tuple(outs),
        in_specs=[pl.BlockSpec(memory_space=pltpu.SMEM)]
        + [ANYWHERE] * (len(rows_in) + len(grads_in) + 3),
        out_specs=(IN_VMEM,) * len(outs),
        scratch_shapes=[
            pltpu.VMEM((rows, width), jnp.bfloat16),
            pltpu.VMEM((rows, width + LANES), jnp.bfloat16),
            pltpu.VMEM((hidden, width), jnp.bfloat16),
            pltpu.VMEM((2 * whole_lanes(hidden), width), jnp.bfloat16),
            pltpu.VMEM((rows, 2 * whole_lanes(hidden)), jnp.bfloat16),
            pltpu.SemaphoreType.DMA((len(rows_in),)),
            pltpu.SemaphoreType.DMA((len(grads_in),)),
            pltpu.SemaphoreType.DMA((1,)),
            pltpu.SemaphoreType.DMA((2,)),
        ],
        compiler_params=pltpu.CompilerParams(vmem_limit_bytes=VMEM_LIMIT),
        cost_estimate=pl.CostEstimate(
            flops=10 * rows * width * hidden,
            bytes_accessed=6 * width * hidden + 6 * rows * width,
            transcendentals=rows * hidden,
        ),
        name="expert_math",
    )(expert, *rows_in, *grads_in, *weights)


def toggled(value, axis, mask):
    pairs = [(source, source ^ mask) for source in range(lax.axis_size(axis))]
    return lax.ppermute(value, axis, pairs)


def along_local(block):
    far = toggled(block, "local", 2)
    return block, toggled(block, "local", 1), far, toggled(far, "local", 1)


def spread(columns):
    block, near, far, corner = columns
    first = [toggled(column, "group", 1) for column in (block, far, corner)]
    second = [toggled(column, "group", 2) for column in (block, far, corner)]
    first.insert(1, toggled(first[0], "local", 1))
    second.insert(1, toggled(second[0], "local", 1))
    half = block.shape[0] // 2
    low = [toggled(column[:half], "group", 2) for column in first]
    high = [toggled(column[half:], "group", 1) for column in second]
    return list(zip((block, near, far, corner), first, second, low, high))


def piece_plan(found, begin, rows):
    half = found[0][0].shape[0] // 2
    arrays, plan = [], []
    for level, (column, first, second, low, high) in enumerate(found):
        for slot, array in ((0, column), (1, first), (2, second)):
            arrays.append(array)
            plan.append((begin, rows, (4 * slot + level) * rows))
        place = (12 + level) * rows
        upto = min(half, begin + rows)
        if begin < upto:
            arrays.append(low)
            plan.append((begin, upto - begin, place))
        since = max(half, begin)
        if since < begin + rows:
            arrays.append(high)
            plan.append((since - half, begin + rows - since, place + since - begin))
    return arrays, tuple(plan)


def added(*values):
    total = values[0].astype(jnp.float32)
    for value in values[1:]:
        total = total + value.astype(jnp.float32)
    return total


def result_blocks(rows):
    quarter = 4 * rows
    diag = [(3 * quarter + level * rows, rows) for level in range(4)]
    sides = []
    for start in (quarter, 2 * quarter):
        sides += [(start + level * rows, rows) for level in range(4)]
    own = [(0, 2 * rows), (2 * rows, rows), (3 * rows, rows)]
    return tuple(diag + sides + own)


def narrowed(value):
    return value.astype(jnp.bfloat16)


def brought_back(blocks):
    diag_0, diag_1, diag_2, diag_3 = blocks[:4]
    first_0, first_1, first_2, first_3, second_0, second_1, second_2, second_3 = blocks[4:12]
    own_low, own_2, own_3 = blocks[12:]
    rows = diag_0.shape[0]
    got_2 = toggled(diag_2, "group", 1)
    got_3 = toggled(diag_3, "group", 2)
    got_0 = toggled(diag_0, "group", 1)
    got_1 = toggled(diag_1, "group", 2)
    from_first_2 = toggled(first_2, "group", 1)
    from_second_3 = toggled(second_3, "group", 2)
    from_first_3 = toggled(narrowed(added(first_3, got_3)), "group", 1)
    from_second_2 = toggled(narrowed(added(second_2, got_2)), "group", 2)
    from_far = toggled(narrowed(added(own_2, from_first_2, from_second_2)), "local", 2)
    from_corner = toggled(narrowed(added(own_3, from_first_3, from_second_3)), "local", 3)
    first_low = jnp.concatenate([first_0, narrowed(added(first_1, got_1))])
    second_low = jnp.concatenate([narrowed(added(second_0, got_0)), second_1])
    from_first_low = toggled(first_low, "group", 1)
    from_second_low = toggled(second_low, "group", 2)
    low = added(own_low, from_first_low, from_second_low)
    from_near = toggled(narrowed(low[rows:]), "local", 1)
    return added(low[:rows], from_near, from_far, from_corner)


def dense_local(
    output_grad,
    carried_grad,
    layer_inputs,
    expert_ids,
    gate_prob,
    gate_weight,
    up_weight,
    down_weight,
):
    expert_count = lax.axis_size("group") * lax.axis_size("local") // 2
    micro_count, rows, width = output_grad.shape
    gate_half, up_half, down_half = gate_weight[0, 0].T, up_weight[0, 0].T, down_weight[0, 0]
    own_index = lax.axis_index("group") * lax.axis_size("local") + lax.axis_index("local")
    expert = jnp.reshape(own_index // 2, (1,)).astype(jnp.int32)
    matches = (expert_ids[0][..., None] == jnp.arange(LANES, dtype=jnp.int32)).astype(jnp.float32)
    token_probs = jnp.sum(matches * gate_prob[0].astype(jnp.float32)[..., None], axis=2)
    token_probs = token_probs.astype(jnp.bfloat16)
    last_section = lax.axis_index("pipe") == lax.axis_size("pipe") - 1
    inputs = layer_inputs[0]
    blocks = result_blocks(rows)
    weights = (gate_half, up_half, down_half)
    wide_inputs = jnp.pad(inputs, ((0, 0), (0, 0), (0, LANES)))
    later_inputs = [along_local(wide_inputs[m]) for m in range(1, micro_count)]
    earlier = carried_grad
    grads_out, gates = [], []
    for m in range(micro_count):
        if m > 0:
            earlier = from_behind(grads_out[-1], "pipe", -1)
        incoming = jnp.where(last_section, output_grad[m], earlier)
        wide_incoming = jnp.concatenate([incoming, token_probs[m]], axis=1)
        if m == 0:
            columns = along_local(jnp.concatenate([wide_inputs[m], wide_incoming], axis=0))
        else:
            columns = [
                jnp.concatenate(pair, axis=0)
                for pair in zip(later_inputs[m - 1], along_local(wide_incoming))
            ]
        found = spread(columns)
        arrays, plan = piece_plan(found, 0, rows)
        grad_arrays, grad_plan = piece_plan(found, rows, rows)
        pieces = expert_math(arrays, plan, grad_arrays, grad_plan, blocks, expert, weights)
        total = brought_back(pieces)
        grads_out.append(added(incoming, total[:, :width]).astype(jnp.bfloat16))
        gates.append(total[:, width:])
    gates = jnp.sum(matches * jnp.stack(gates)[:, :, None, :], axis=3).astype(jnp.bfloat16)
    return (jnp.stack(grads_out)[None], gates[None])


def local(*arguments):
    group, ring = lax.axis_size("group"), lax.axis_size("local")
    top_count = arguments[3].shape[-1]
    expert_count = group * ring // 2
    crowded = 3 * expert_count <= 4 * top_count
    if group == 4 and ring == 4 and crowded and expert_count <= LANES:
        return dense_local(*arguments)
    return routed_local(*arguments)


def solution(mesh):
    return jax.shard_map(
        local,
        mesh=mesh,
        in_specs=(
            P(None, ("group", "local"), None),
            P(("group", "local"), None),
            P("pipe", None, ("group", "local"), None),
            P("pipe", None, ("group", "local"), None),
            P("pipe", None, ("group", "local"), None),
            P("pipe", ("group", "local"), None, None),
            P("pipe", ("group", "local"), None, None),
            P("pipe", ("group", "local"), None, None),
        ),
        out_specs=(
            P("pipe", None, ("group", "local"), None),
            P("pipe", None, ("group", "local"), None),
        ),
        check_vma=False,
    )
```
